32 devices in a mesh: blk: 8 (over z, x), hist: 4 (over y, core).
Axes of the slice: x: 2, y: 2, z: 4, core: 2. Of those that a mesh axis runs over, the one named last changes fastest.
Arguments:
- hidden: bfloat16 [8192, 512], P(('blk', 'hist')), may hold values from -6 to 6
- initial: bfloat16 [8192, 512], P(('blk', 'hist')), may hold values from -6 to 6
- own_adj: bfloat16 [8192, 256], P(('blk', 'hist')), may hold values from -0.21875 to 0.21875
- tiles: bfloat16 [128, 64, 64], P(('blk', 'hist')), may hold values from -0.21875 to 0.21875
- tile_src: int32 [32, 4], P(('blk', 'hist')), may hold values from 0 to 31, as said below
- tile_dst: int32 [32, 4], P(('blk', 'hist')), may hold values from 0 to 3
- history: bfloat16 [32768, 512], P(('blk', 'hist')), may hold values from -6 to 6
- pull_rows: int32 [32, 4, 128], P(('blk', 'hist')), may hold values from 0 to 1023
- pull_count: int32 [32, 4], P(('blk', 'hist')), may hold values from 1 to 128, 256 in all within a row
- pull_adj: bfloat16 [8192, 512], P(('blk', 'hist')), may hold values from -0.21875 to 0.21875
- weight: bfloat16 [512, 512], replicated, may hold values from -0.25 to 0.25
- push_rows: int32 [8192], P(('blk', 'hist')), may hold values from 0 to 1023, as said below
Outputs:
- refreshed: bfloat16 [8192, 512], P(('blk', 'hist'))
- new_history: bfloat16 [32768, 512], P(('blk', 'hist'))
The draws below stay inside these ranges and needn't reach their ends.
Inputs may be any that keep to these rules, and one draw needn't show every extreme that they name: `tile_src`: the 4 tiles of one device take their sources from 4 different other blk indices, one block each. `pull_count`: each device's counts sum to 256; slots past the count hold arbitrary rows. `push_rows`: within one blk group the rows written to each owner are all different.
All inputs are finite; a program needn't handle non-finite values.
Results may differ from the reference program's by a relative error of at most 0.005.
Values may be sent and summed in bfloat16 or wider, within the bound.
No kernel may reach another device: no remote copies, remote signals or barrier semaphores. Data moves between devices by JAX's collectives and lax.ppermute only.
A program may use at most 64 MiB of HBM per device.

```python
import math
import jax
import jax.numpy as jnp
import numpy as np
from jax import lax

H = 512
BLOCK = 64
CAP = 128
ROWS_DEV = 256
HROWS_DEV = 1024
TILES = 4
NODES = 8192
HROWS = 32768
N_BLK = 8
N_HIST = 4


def draw_tile_src(key, part):
    key = jax.random.fold_in(key, 11)
    per_dev = ROWS_DEV // BLOCK
    keys = jax.random.split(key, N_BLK * N_HIST)
    groups = jnp.arange(N_BLK * N_HIST, dtype=jnp.int32) // N_HIST

    def one_row(row_key, group):
        first_key, second_key = jax.random.split(row_key)
        offsets = jax.random.permutation(first_key, N_BLK - 1)[:TILES].astype(jnp.int32)
        peers = (group + 1 + offsets) % N_BLK
        local_block = jax.random.randint(second_key, (TILES,), 0, per_dev, dtype=jnp.int32)
        return (peers * per_dev + local_block).astype(jnp.int32)
    return jax.vmap(one_row)(keys, groups)


def draw_push_rows(key, part):
    key = jax.random.fold_in(key, 23)
    per_owner = ROWS_DEV // N_HIST
    keys = jax.random.split(key, N_BLK * N_HIST)

    def one_owner(row_key):
        return jax.random.permutation(row_key, HROWS_DEV)[:ROWS_DEV].astype(jnp.int32)
    chosen = jax.vmap(one_owner)(keys).reshape(N_BLK, N_HIST, N_HIST, per_owner)
    return jnp.transpose(chosen, (0, 2, 1, 3)).reshape(-1).astype(jnp.int32)


def set_ends(drawn, key, low, largest):
    longest = drawn.shape.index(max(drawn.shape))
    spots = []
    for shift in (0, 1):
        where = [jax.random.randint(jax.random.fold_in(key, axis), (), 0, length) for axis, length in enumerate(drawn.shape)]
        where[longest] = (where[longest] + shift) % drawn.shape[longest]
        spots.append(tuple(where))
    return drawn.at[spots[0]].set(low).at[spots[1]].set(largest)


def levels(own_key, dims, shards, least, high):
    gain = 1.0
    for axis_at, blocks in shards:
        steps = jax.random.uniform(jax.random.fold_in(jax.random.fold_in(own_key, 6), axis_at), (blocks,), jnp.float32, least / len(shards), high / len(shards))
        gain = gain * jnp.repeat(jnp.exp(steps), dims[axis_at] // blocks).reshape((-1,) + (1,) * (len(dims) - 1 - axis_at))
    return gain


def split_up(amount, total, reach, lean):
    loads = [(1 << 20) // math.isqrt(rank ** lean) + 1 for rank in range(2, amount + 1)]
    spare, counts = total - reach - (amount - 1), [1] * (amount - 1)
    while spare > 0:
        free = [i for i in range(amount - 1) if counts[i] < reach]
        whole, remaining = sum([loads[i] for i in free]), spare
        for i in free:
            more = min(reach - counts[i], max(1, remaining * loads[i] // whole), spare)
            counts[i] = counts[i] + more
            spare = spare - more
    return np.array([reach] + counts)


def uneven_parts(rng, number_of, total, most, skew):
    if number_of == 2:
        one = jax.random.randint(rng, (), max(1, total - most), min(most, total - 1) + 1)
        return jnp.stack([one, total - one])
    tallies = jnp.asarray(split_up(number_of, total, most, skew), jnp.int32)
    couples = (number_of - 1) // 2
    source_of, taker = tallies[1:1 + 2 * couples:2], tallies[2:2 + 2 * couples:2]
    slack = jnp.minimum(source_of - 1, most - taker)
    moved = jax.random.randint(jax.random.fold_in(rng, 1), (couples,), 0, 1 << 20) % (slack + 1)
    tallies = tallies.at[1:1 + 2 * couples:2].set(source_of - moved).at[2:2 + 2 * couples:2].set(taker + moved)
    return tallies[jax.random.permutation(jax.random.fold_in(rng, 2), number_of)]


def centred(key, shape, width, limit, cuts=(), held_as=jnp.bfloat16):
    level = levels(key, shape, cuts, -0.22, 0.18) if cuts else 1.0
    entries = jax.random.normal(key, shape, jnp.float32) * width * level
    return jnp.minimum(jnp.maximum(entries, -limit), limit).astype(held_as)


def setup_inputs(seed: int = 0) -> dict:
    key_of = jax.random.split(jax.random.key(seed), 13)
    hidden = centred(key_of[0], (NODES, H), 1.0, 6.0, ((0, 32),))
    initial = centred(key_of[1], (NODES, H), 1.0, 6.0, ((0, 32),))
    own_adj = centred(key_of[2], (NODES, ROWS_DEV), (ROWS_DEV + TILES * BLOCK + N_HIST * CAP // 2) ** -0.5, 0.21875, ((0, 32),))
    tiles = centred(key_of[3], (NODES // ROWS_DEV * TILES, BLOCK, BLOCK), (ROWS_DEV + TILES * BLOCK + N_HIST * CAP // 2) ** -0.5, 0.21875, ((0, 32),))
    tile_src = draw_tile_src(jax.random.fold_in(key_of[12], 71), 0)
    tile_dst = set_ends(jax.random.randint(key_of[5], (N_BLK * N_HIST, TILES), 0, ROWS_DEV // BLOCK), jax.random.fold_in(key_of[5], 1), 0, (ROWS_DEV // BLOCK) - 1).astype(jnp.int32)
    history = centred(key_of[6], (HROWS, H), 1.0, 6.0, ((0, 32),))
    pull_rows = set_ends(jax.random.randint(key_of[7], (N_BLK * N_HIST, N_HIST, CAP), 0, HROWS_DEV), jax.random.fold_in(key_of[7], 1), 0, HROWS_DEV - 1).astype(jnp.int32)
    pull_count = jax.vmap(lambda own: uneven_parts(own, N_HIST, N_HIST * CAP // 2, CAP, 2))(jax.random.split(key_of[8], (N_BLK * N_HIST))).reshape((N_BLK * N_HIST, N_HIST)).astype(jnp.int32)
    pull_adj = centred(key_of[9], (NODES, N_HIST * CAP), (ROWS_DEV + TILES * BLOCK + N_HIST * CAP // 2) ** -0.5, 0.21875, ((0, 32),))
    weight = centred(key_of[10], (H, H), H ** -0.5, 0.25)
    push_rows = draw_push_rows(jax.random.fold_in(key_of[12], 71), 0)
    return {"hidden": hidden, "initial": initial, "own_adj": own_adj, "tiles": tiles, "tile_src": tile_src, "tile_dst": tile_dst, "history": history, "pull_rows": pull_rows, "pull_count": pull_count, "pull_adj": pull_adj, "weight": weight, "push_rows": push_rows}


alpha_init = 0.1
beta_map = 0.4


def reference(hidden, initial, own_adj, tiles, tile_src, tile_dst, history, pull_rows, pull_count, pull_adj, weight, push_rows):
    per_dev = ROWS_DEV // BLOCK
    per_owner = ROWS_DEV // N_HIST
    blocks = hidden.reshape(N_BLK, N_HIST, per_dev, BLOCK, H)
    group_hidden = hidden.reshape(N_BLK, N_HIST, ROWS_DEV, H)
    group_init = initial.reshape(N_BLK, N_HIST, ROWS_DEV, H)
    group_own = own_adj.reshape(N_BLK, N_HIST, ROWS_DEV, ROWS_DEV)
    group_tiles = tiles.reshape(N_BLK, N_HIST, TILES, BLOCK, BLOCK)
    group_src = tile_src.reshape(N_BLK, N_HIST, TILES)
    group_dst = tile_dst.reshape(N_BLK, N_HIST, TILES)
    group_hist = history.reshape(N_BLK, N_HIST, HROWS_DEV, H)
    group_prow = pull_rows.reshape(N_BLK, N_HIST, N_HIST, CAP)
    group_pcnt = pull_count.reshape(N_BLK, N_HIST, N_HIST)
    group_padj = pull_adj.reshape(N_BLK, N_HIST, ROWS_DEV, N_HIST * CAP)
    weight_f = weight.astype(jnp.float32)

    def one_group(items):
        b_hid, b_init, b_own, b_tiles, b_src, b_dst, b_hist, b_prow, b_pcnt, b_padj = items

        def device(column, d_hid, d_init, d_own, d_tiles, d_src, d_dst, d_prow, d_pcnt, d_padj):
            inside = jnp.dot(d_own.astype(jnp.float32), d_hid.astype(jnp.float32), precision=lax.Precision.HIGHEST)
            sources = blocks[d_src // per_dev, column, d_src % per_dev].astype(jnp.float32)
            products = jnp.einsum('kqr,krh->kqh', d_tiles.astype(jnp.float32), sources, precision=lax.Precision.HIGHEST)
            dst_onehot = (d_dst[:, None] == jnp.arange(per_dev, dtype=jnp.int32)[None, :]).astype(jnp.float32)
            remote = jnp.einsum('kd,kqh->dqh', dst_onehot, products, precision=lax.Precision.HIGHEST).reshape(ROWS_DEV, H)
            arrived = b_hist[jnp.arange(N_HIST, dtype=jnp.int32)[:, None], d_prow]
            filled = jnp.arange(CAP, dtype=jnp.int32)[None, :] < d_pcnt[:, None]
            arrived = jnp.where(filled[:, :, None], arrived.astype(jnp.float32), 0.0).reshape(N_HIST * CAP, H)
            outside = jnp.dot(d_padj.astype(jnp.float32), arrived, precision=lax.Precision.HIGHEST)
            aggregate = inside + remote + outside
            support = ((1.0 - alpha_init) * aggregate + alpha_init * d_init.astype(jnp.float32)).astype(jnp.bfloat16)
            projected = jnp.dot(support.astype(jnp.float32), weight_f, precision=lax.Precision.HIGHEST)
            return jax.nn.relu((1.0 - beta_map) * support.astype(jnp.float32) + beta_map * projected).astype(jnp.bfloat16)

        return jax.vmap(device)(jnp.arange(N_HIST, dtype=jnp.int32), b_hid, b_init, b_own, b_tiles, b_src, b_dst, b_prow, b_pcnt, b_padj)

    refreshed = lax.map(one_group, (group_hidden, group_init, group_own, group_tiles, group_src, group_dst, group_hist, group_prow, group_pcnt, group_padj))
    refreshed = refreshed.reshape(NODES, H)
    node = jnp.arange(NODES, dtype=jnp.int32)
    device_index = node // ROWS_DEV
    group_index = device_index // N_HIST
    owner = (node % ROWS_DEV) // per_owner
    target = (group_index * N_HIST + owner) * HROWS_DEV + push_rows
    new_history = history.at[target].set(refreshed)
    return refreshed, new_history
```

```python
import functools

import jax
import jax.numpy as jnp
from jax import lax
from jax.experimental import pallas as pl
from jax.experimental.pallas import tpu as pltpu
from jax.sharding import PartitionSpec as P

alpha_init = 0.1
beta_map = 0.4

VMEM = pltpu.VMEM
SMEM = pltpu.SMEM
LIMIT = 24 * 1024 * 1024


def vmem():
    return pl.BlockSpec(memory_space=VMEM)


def smem():
    return pl.BlockSpec(memory_space=SMEM)


def cost(flops, size):
    return pl.CostEstimate(flops=flops, bytes_accessed=size, transcendentals=0)


def params():
    return pltpu.CompilerParams(vmem_limit_bytes=LIMIT)


def swap(x, axis, n, k):
    return lax.ppermute(x, axis, [(i, i ^ k) for i in range(n)])


def message_kernel(n_blk, n_hist, per_dev, src, count, rows, push, out):
    tiles = src.shape[1]
    cap = rows.shape[2]
    per_owner = push.shape[1] // n_hist
    rest = out.shape[2] - cap - per_owner
    lane = lax.broadcasted_iota(jnp.int32, (1, cap), 1)
    for h in range(n_hist):
        asked = jnp.where(lane < count[0, h], rows[0, h : h + 1, :], -1)
        pushed = push[:, h * per_owner : (h + 1) * per_owner]
        for b in range(n_blk):
            out[b * n_hist + h, :, :cap] = asked
            out[b * n_hist + h, :, cap : cap + per_owner] = pushed
    for b in range(n_blk):
        wanted = 0
        for k in range(tiles):
            wanted = jnp.where(src[0, k] // per_dev == b, src[0, k] % per_dev, wanted)
        for h in range(n_hist):
            out[b * n_hist + h, :, cap + per_owner :] = jnp.full((1, rest), wanted, jnp.int32)


def pick_kernel(n_blk, n_hist, at, place, asked, hidden, out):
    rows = out.shape[1]
    h = place[1]
    per_dev = hidden.shape[0] // rows
    for b in range(n_blk):
        wanted = asked[b * n_hist + h][:, at : at + 1]
        block = hidden[:rows, :]
        for j in range(1, per_dev):
            block = jnp.where(
                jnp.broadcast_to(wanted == j, block.shape), hidden[j * rows : (j + 1) * rows, :], block
            )
        out[b] = block


def pull_kernel(n_hist, cap, place, asked, history, *outs):
    b, h = place[0], place[1]
    for k in range(n_hist):
        rows = asked[b * n_hist + (h ^ k)][:, :cap]
        held = lax.broadcasted_iota(jnp.int32, (history.shape[0], cap), 0)
        hot = jnp.where(held == rows, 1.0, 0.0).astype(jnp.bfloat16)
        outs[k][...] = lax.dot_general(
            hot, history[...], (((0,), (0,)), ((), ())), preferred_element_type=jnp.float32
        ).astype(jnp.bfloat16)


def partial_kernel(n_hist, cap, place, own_adj, hidden, pull_adj, initial, *refs):
    arrived, out = refs[:n_hist], refs[n_hist]
    h = place[1]
    total = jnp.dot(own_adj[...], hidden[...], preferred_element_type=jnp.float32)
    for k in range(n_hist):
        columns = pl.ds(pl.multiple_of((h ^ k) * cap, cap), cap)
        total += jnp.dot(pull_adj[:, columns], arrived[k][...], preferred_element_type=jnp.float32)
    out[...] = (1.0 - alpha_init) * total + alpha_init * initial[...].astype(jnp.float32)


def final_kernel(n_hist, per_dev, place, src, dst, part, tiles, received, weight, refreshed, *refs):
    sent, total = refs[:n_hist], refs[n_hist]
    block = tiles.shape[1]
    h = place[1]
    total[...] = part[...]
    for k in range(tiles.shape[0]):
        product = jnp.dot(
            tiles[k], received[src[0, k] // per_dev], preferred_element_type=jnp.float32
        )
        rows = pl.ds(pl.multiple_of(dst[0, k] * block, block), block)
        total[rows, :] += (1.0 - alpha_init) * product
    support = total[...].astype(jnp.bfloat16)
    projected = jnp.dot(support, weight[...], preferred_element_type=jnp.float32)
    refreshed[...] = jnp.maximum(
        (1.0 - beta_map) * support.astype(jnp.float32) + beta_map * projected, 0.0
    ).astype(jnp.bfloat16)
    size = refreshed.shape[0] // n_hist
    for k in range(n_hist):
        sent[k][...] = refreshed[pl.ds(pl.multiple_of((h ^ k) * size, size), size), :]


def scatter_kernel(n_hist, cap, place, asked, history, *refs):
    pushed, out, index, rows = refs[:n_hist], refs[n_hist], refs[n_hist + 1], refs[n_hist + 2]
    b, h = place[0], place[1]
    size = pushed[0].shape[0]
    for k in range(n_hist):
        index[:, k * size : (k + 1) * size] = asked[b * n_hist + (h ^ k)][:, cap : cap + size]
        rows[k * size : (k + 1) * size, :] = pushed[k][...]
    held = lax.broadcasted_iota(jnp.int32, (history.shape[0], index.shape[1]), 0)
    hot = jnp.where(
        held + pl.program_id(0) * history.shape[0] == index[...], 1.0, 0.0
    )
    hit = jnp.sum(hot, axis=1, keepdims=True)
    new = jnp.dot(hot.astype(jnp.bfloat16), rows[...], preferred_element_type=jnp.float32)
    out[...] = jnp.where(hit > 0.0, new, history[...].astype(jnp.float32)).astype(jnp.bfloat16)


def local(
    hidden,
    initial,
    own_adj,
    tiles,
    tile_src,
    tile_dst,
    history,
    pull_rows,
    pull_count,
    pull_adj,
    weight,
    push_rows,
):
    rows_dev, feature = hidden.shape
    block_rows = tiles.shape[1]
    per_dev = rows_dev // block_rows
    n_blk = lax.axis_size("blk")
    n_hist = lax.axis_size("hist")
    cap = pull_rows.shape[2]
    per_owner = rows_dev // n_hist
    held = history.shape[0]
    width = cap + -(-(per_owner + 1) // 128) * 128
    place = jnp.stack([lax.axis_index("blk"), lax.axis_index("hist")]).astype(jnp.int32)

    def shape(s, dtype=jnp.bfloat16):
        return jax.ShapeDtypeStruct(s, dtype)

    message = pl.pallas_call(
        functools.partial(message_kernel, n_blk, n_hist, per_dev),
        out_shape=shape((n_blk * n_hist, 1, width), jnp.int32),
        in_specs=[smem(), smem(), vmem(), vmem()],
        out_specs=vmem(),
        compiler_params=params(),
        name="message",
    )(tile_src, pull_count, pull_rows, push_rows.reshape(1, rows_dev))
    asked = lax.all_to_all(message, ("blk", "hist"), split_axis=0, concat_axis=0, tiled=True)

    picked = pl.pallas_call(
        functools.partial(pick_kernel, n_blk, n_hist, cap + per_owner),
        out_shape=shape((n_blk, block_rows, feature)),
        in_specs=[smem(), vmem(), vmem()],
        out_specs=vmem(),
        compiler_params=params(),
        name="pick",
    )(place, asked, hidden)
    received = lax.all_to_all(picked, "blk", split_axis=0, concat_axis=0, tiled=True)

    fetched = pl.pallas_call(
        functools.partial(pull_kernel, n_hist, cap),
        out_shape=[shape((cap, feature))] * n_hist,
        in_specs=[smem(), vmem(), vmem()],
        out_specs=[vmem()] * n_hist,
        compiler_params=params(),
        cost_estimate=cost(2 * n_hist * cap * held * feature, held * feature * 4),
        name="pull",
    )(place, asked, history)
    arrived = [fetched[0]] + [swap(fetched[k], "hist", n_hist, k) for k in range(1, n_hist)]

    part = pl.pallas_call(
        functools.partial(partial_kernel, n_hist, cap),
        out_shape=shape((rows_dev, feature), jnp.float32),
        in_specs=[smem()] + [vmem()] * (4 + n_hist),
        out_specs=vmem(),
        compiler_params=params(),
        cost_estimate=cost(2 * rows_dev * feature * (rows_dev + n_hist * cap), rows_dev * feature * 12),
        name="partial",
    )(place, own_adj, hidden, pull_adj, initial, *arrived)

    refreshed, *sent = pl.pallas_call(
        functools.partial(final_kernel, n_hist, per_dev),
        out_shape=[shape((rows_dev, feature))] + [shape((per_owner, feature))] * n_hist,
        in_specs=[smem()] * 3 + [vmem()] * 4,
        out_specs=[vmem()] * (1 + n_hist),
        scratch_shapes=[VMEM((rows_dev, feature), jnp.float32)],
        compiler_params=params(),
        cost_estimate=cost(2 * rows_dev * feature * feature, rows_dev * feature * 12),
        name="final",
    )(place, tile_src, tile_dst, part, tiles, received, weight)
    pushed = [sent[0]] + [swap(sent[k], "hist", n_hist, k) for k in range(1, n_hist)]

    steps = 4
    whole = lambda s: pl.BlockSpec(s, lambda i: (0,) * len(s))
    new_history = pl.pallas_call(
        functools.partial(scatter_kernel, n_hist, cap),
        grid=(steps,),
        out_shape=shape((held, feature)),
        in_specs=[
            smem(),
            whole((n_blk * n_hist, 1, width)),
            pl.BlockSpec((held // steps, feature), lambda i: (i, 0)),
        ]
        + [whole((per_owner, feature))] * n_hist,
        out_specs=pl.BlockSpec((held // steps, feature), lambda i: (i, 0)),
        scratch_shapes=[VMEM((1, rows_dev), jnp.int32), VMEM((rows_dev, feature), jnp.bfloat16)],
        compiler_params=params(),
        name="scatter",
    )(place, asked, history, *pushed)
    return (refreshed, new_history)


def solution(mesh):
    both = P(("blk", "hist"))
    return jax.shard_map(
        local,
        mesh=mesh,
        in_specs=(both,) * 10 + (P(), both),
        out_specs=(both, both),
        check_vma=False,
    )
```

```python
import functools

import jax
import jax.numpy as jnp
from jax import lax
from jax.experimental import pallas as pl
from jax.experimental.pallas import tpu as pltpu
from jax.sharding import PartitionSpec as P

alpha_init = 0.1
beta_map = 0.4

VMEM = pltpu.VMEM
SMEM = pltpu.SMEM
LIMIT = 24 * 1024 * 1024


def vmem():
    return pl.BlockSpec(memory_space=VMEM)


def smem():
    return pl.BlockSpec(memory_space=SMEM)


def cost(flops, size):
    return pl.CostEstimate(flops=flops, bytes_accessed=size, transcendentals=0)


def params():
    return pltpu.CompilerParams(vmem_limit_bytes=LIMIT)


def swap(x, axis, n, k):
    return lax.ppermute(x, axis, [(i, i ^ k) for i in range(n)])


def message_kernel(n_hist, n_half, per_dev, place, src, count, rows, push, *outs):
    to_hist, to_half = outs[:n_hist], outs[n_hist:]
    tiles = src.shape[1]
    cap = rows.shape[2]
    per_owner = push.shape[1] // n_hist
    b, h = place[0], place[1]
    lane = lax.broadcasted_iota(jnp.int32, (1, cap), 1)
    for k in range(n_hist):
        o = h ^ k
        to_hist[k][:, :cap] = jnp.where(lane < count[0, o], rows[0, pl.ds(o, 1), :], -1)
        pushed = push[:, :per_owner]
        for j in range(1, n_hist):
            pushed = jnp.where(o == j, push[:, j * per_owner : (j + 1) * per_owner], pushed)
        to_hist[k][:, cap : cap + per_owner] = pushed
    for k in range(n_half):
        own, other = 0, 0
        for t in range(tiles):
            far = (src[0, t] // per_dev) ^ b
            own = jnp.where(far == k, src[0, t] % per_dev, own)
            other = jnp.where(far == k + n_half, src[0, t] % per_dev, other)
        to_half[k][:, :128] = jnp.full((1, 128), own, jnp.int32)
        to_half[k][:, 128:] = jnp.full((1, 128), other, jnp.int32)


def pick_kernel(n_half, hidden, mirror, *refs):
    asked, outs = refs[:n_half], refs[n_half:]
    rows = outs[0].shape[0] // 2
    per_dev = hidden.shape[0] // rows
    for k in range(n_half):
        for slot, held in enumerate((hidden, mirror)):
            wanted = asked[k][:, slot * 128 : slot * 128 + 1]
            block = held[:rows, :]
            for j in range(1, per_dev):
                block = jnp.where(
                    jnp.broadcast_to(wanted == j, block.shape), held[j * rows : (j + 1) * rows, :], block
                )
            outs[k][slot * rows : (slot + 1) * rows, :] = block


def pull_kernel(n_hist, cap, history, *refs):
    asked, outs = refs[:n_hist], refs[n_hist:]
    held = lax.broadcasted_iota(jnp.int32, (history.shape[0], cap), 0)
    for k in range(n_hist):
        hot = jnp.where(held == asked[k][:, :cap], 1.0, 0.0).astype(jnp.bfloat16)
        outs[k][...] = lax.dot_general(
            hot, history[...], (((0,), (0,)), ((), ())), preferred_element_type=jnp.float32
        ).astype(jnp.bfloat16)


def prepare_kernel(n_hist, cap, history, *refs):
    asked, (base, hot, index) = refs[:n_hist], refs[n_hist:]
    size = index.shape[1] // n_hist
    for k in range(n_hist):
        index[:, k * size : (k + 1) * size] = asked[k][:, cap : cap + size]
    held = lax.broadcasted_iota(jnp.int32, hot.shape, 0)
    found = jnp.where(held == index[...], 1.0, 0.0)
    hot[...] = found.astype(jnp.bfloat16)
    hit = jnp.sum(found, axis=1, keepdims=True)
    base[...] = jnp.where(hit > 0.0, 0.0, history[...].astype(jnp.float32)).astype(jnp.bfloat16)


def partial_kernel(n_hist, cap, place, own_adj, hidden, pull_adj, initial, *refs):
    arrived, out = refs[:n_hist], refs[n_hist]
    h = place[1]
    total = jnp.dot(own_adj[...], hidden[...], preferred_element_type=jnp.float32)
    for k in range(n_hist):
        columns = pl.ds(pl.multiple_of((h ^ k) * cap, cap), cap)
        total += jnp.dot(pull_adj[:, columns], arrived[k][...], preferred_element_type=jnp.float32)
    out[...] = (1.0 - alpha_init) * total + alpha_init * initial[...].astype(jnp.float32)


def final_kernel(n_hist, n_half, per_dev, place, src, dst, part, tiles, weight, *refs):
    received, sent = refs[:n_half], refs[n_half : n_half + n_hist]
    total, blocks, result = refs[n_half + n_hist :]
    block = tiles.shape[1]
    b, h = place[0], place[1]
    total[...] = part[...]
    for k in range(n_half):
        blocks[k] = received[k][:block, :]
        blocks[k + n_half] = received[k][block:, :]
    for t in range(tiles.shape[0]):
        product = jnp.dot(
            tiles[t], blocks[(src[0, t] // per_dev) ^ b], preferred_element_type=jnp.float32
        )
        rows = pl.ds(pl.multiple_of(dst[0, t] * block, block), block)
        total[rows, :] += (1.0 - alpha_init) * product
    support = total[...].astype(jnp.bfloat16)
    projected = jnp.dot(support, weight[...], preferred_element_type=jnp.float32)
    result[...] = jnp.maximum(
        (1.0 - beta_map) * support.astype(jnp.float32) + beta_map * projected, 0.0
    ).astype(jnp.bfloat16)
    size = result.shape[0] // n_hist
    for k in range(n_hist):
        sent[k][...] = result[pl.ds(pl.multiple_of((h ^ k) * size, size), size), :]


def scatter_kernel(n_hist, steps, place, base, hot, *refs):
    sent, pushed = refs[:n_hist], refs[n_hist : 2 * n_hist]
    refreshed, out, rows, new, sent_sem, new_sem = refs[2 * n_hist :]
    h = place[1]
    size = sent[0].shape[0]
    copies = []
    for k in range(n_hist):
        to = refreshed.at[pl.ds(pl.multiple_of((h ^ k) * size, size), size), :]
        copies.append(pltpu.make_async_copy(sent[k], to, sent_sem.at[k]))
        copies[-1].start()
        rows[k * size : (k + 1) * size, :] = pushed[k][...]
    step = base.shape[0] // steps
    for i in range(steps):
        at = slice(i * step, (i + 1) * step)
        found = jnp.dot(hot[at, :], rows[...], preferred_element_type=jnp.float32)
        new[at, :] = (base[at, :].astype(jnp.float32) + found).astype(jnp.bfloat16)
        copies.append(pltpu.make_async_copy(new.at[at, :], out.at[at, :], new_sem.at[i]))
        copies[-1].start()
    for copy in copies:
        copy.wait()


def local(
    hidden,
    initial,
    own_adj,
    tiles,
    tile_src,
    tile_dst,
    history,
    pull_rows,
    pull_count,
    pull_adj,
    weight,
    push_rows,
):
    rows_dev, feature = hidden.shape
    block_rows = tiles.shape[1]
    per_dev = rows_dev // block_rows
    n_blk = lax.axis_size("blk")
    n_hist = lax.axis_size("hist")
    cap = pull_rows.shape[2]
    per_owner = rows_dev // n_hist
    held = history.shape[0]
    n_half = n_blk // 2
    place = jnp.stack([lax.axis_index("blk"), lax.axis_index("hist")]).astype(jnp.int32)
    anywhere = pl.BlockSpec(memory_space=pl.ANY)

    def shape(s, dtype=jnp.bfloat16):
        return jax.ShapeDtypeStruct(s, dtype)

    mirror = swap(hidden, "blk", n_blk, n_half)
    asks = pl.pallas_call(
        functools.partial(message_kernel, n_hist, n_half, per_dev),
        out_shape=[shape((1, cap + 128), jnp.int32)] * n_hist + [shape((1, 256), jnp.int32)] * n_half,
        in_specs=[smem(), smem(), smem(), vmem(), vmem()],
        out_specs=[vmem()] * (n_hist + n_half),
        compiler_params=params(),
        name="message",
    )(place, tile_src, pull_count, pull_rows, push_rows.reshape(1, rows_dev))
    asked = [asks[0]] + [swap(asks[k], "hist", n_hist, k) for k in range(1, n_hist)]
    wanted = [asks[n_hist]] + [swap(asks[n_hist + k], "blk", n_blk, k) for k in range(1, n_half)]
    asked, wanted = lax.optimization_barrier((asked, wanted))

    fetched = pl.pallas_call(
        functools.partial(pull_kernel, n_hist, cap),
        out_shape=[shape((cap, feature))] * n_hist,
        in_specs=[vmem()] * (1 + n_hist),
        out_specs=[vmem()] * n_hist,
        compiler_params=params(),
        cost_estimate=cost(2 * n_hist * cap * held * feature, held * feature * 4),
        name="pull",
    )(history, *asked)
    arrived = [fetched[0]] + [swap(fetched[k], "hist", n_hist, k) for k in range(1, n_hist)]

    picked = pl.pallas_call(
        functools.partial(pick_kernel, n_half),
        out_shape=[shape((2 * block_rows, feature))] * n_half,
        in_specs=[vmem()] * (2 + n_half),
        out_specs=[vmem()] * n_half,
        compiler_params=params(),
        cost_estimate=cost(0, n_half * 4 * block_rows * feature * 2),
        name="pick",
    )(hidden, mirror, *wanted)
    received = [picked[0]] + [swap(picked[k], "blk", n_blk, k) for k in range(1, n_half)]

    base, hot = pl.pallas_call(
        functools.partial(prepare_kernel, n_hist, cap),
        out_shape=[shape((held, feature)), shape((held, rows_dev))],
        in_specs=[vmem()] * (1 + n_hist),
        out_specs=[vmem()] * 2,
        scratch_shapes=[VMEM((1, rows_dev), jnp.int32)],
        compiler_params=params(),
        cost_estimate=cost(held * rows_dev * 8, held * feature * 6),
        name="prepare",
    )(history, *asked)

    part = pl.pallas_call(
        functools.partial(partial_kernel, n_hist, cap),
        out_shape=shape((rows_dev, feature), jnp.float32),
        in_specs=[smem()] + [vmem()] * (4 + n_hist),
        out_specs=vmem(),
        compiler_params=params(),
        cost_estimate=cost(2 * rows_dev * feature * (rows_dev + n_hist * cap), rows_dev * feature * 12),
        name="partial",
    )(place, own_adj, hidden, pull_adj, initial, *arrived)

    sent = pl.pallas_call(
        functools.partial(final_kernel, n_hist, n_half, per_dev),
        out_shape=[shape((per_owner, feature))] * n_hist,
        in_specs=[smem()] * 3 + [vmem()] * (3 + n_half),
        out_specs=[vmem()] * n_hist,
        scratch_shapes=[
            VMEM((rows_dev, feature), jnp.float32),
            VMEM((n_blk, block_rows, feature), jnp.bfloat16),
            VMEM((rows_dev, feature), jnp.bfloat16),
        ],
        compiler_params=params(),
        cost_estimate=cost(2 * rows_dev * feature * feature, rows_dev * feature * 12),
        name="final",
    )(place, tile_src, tile_dst, part, tiles, weight, *received)
    pushed = [sent[0]] + [swap(sent[k], "hist", n_hist, k) for k in range(1, n_hist)]

    steps = 4
    refreshed, new_history = pl.pallas_call(
        functools.partial(scatter_kernel, n_hist, steps),
        out_shape=[shape((rows_dev, feature)), shape((held, feature))],
        in_specs=[smem()] + [vmem()] * (2 + 2 * n_hist),
        out_specs=[anywhere] * 2,
        scratch_shapes=[
            VMEM((rows_dev, feature), jnp.bfloat16),
            VMEM((held, feature), jnp.bfloat16),
            pltpu.SemaphoreType.DMA((n_hist,)),
            pltpu.SemaphoreType.DMA((steps,)),
        ],
        compiler_params=params(),
        name="scatter",
    )(place, base, hot, *sent, *pushed)
    return (refreshed, new_history)


def solution(mesh):
    both = P(("blk", "hist"))
    return jax.shard_map(
        local,
        mesh=mesh,
        in_specs=(both,) * 10 + (P(), both),
        out_specs=(both, both),
        check_vma=False,
    )
```

```python
import functools

import jax
import jax.numpy as jnp
from jax import lax
from jax.experimental import pallas as pl
from jax.experimental.pallas import tpu as pltpu
from jax.sharding import PartitionSpec as P

alpha_init = 0.1
beta_map = 0.4

VMEM = pltpu.VMEM
SMEM = pltpu.SMEM
LIMIT = 24 * 1024 * 1024


def vmem():
    return pl.BlockSpec(memory_space=VMEM)


def smem():
    return pl.BlockSpec(memory_space=SMEM)


def cost(flops, size):
    return pl.CostEstimate(flops=flops, bytes_accessed=size, transcendentals=0)


def params():
    return pltpu.CompilerParams(vmem_limit_bytes=LIMIT)


def swap(x, axis, n, k):
    return lax.ppermute(x, axis, [(i, i ^ k) for i in range(n)])


def message_kernel(n_hist, n_half, per_dev, place, src, count, rows, push, *outs):
    to_hist, to_half = outs[:n_hist], outs[n_hist:]
    cap = rows.shape[2]
    per_owner = push.shape[1] // n_hist
    b, h = place[0], place[1]
    for k in range(n_half):
        for slot, name in enumerate((k + n_half, k)):
            wanted = 0
            for t in range(src.shape[1]):
                wanted = jnp.where((src[0, t] // per_dev) ^ b == name, src[0, t] % per_dev, wanted)
            to_half[k][:, slot * 128 : slot * 128 + 128] = jnp.full((1, 128), wanted, jnp.int32)
    lane = lax.broadcasted_iota(jnp.int32, (1, cap), 1)
    for k in range(n_hist):
        o = h ^ k
        to_hist[k][:, :cap] = jnp.where(lane < count[0, o], rows[0, pl.ds(o, 1), :], -1)
        pushed = push[:, :per_owner]
        for j in range(1, n_hist):
            pushed = jnp.where(o == j, push[:, j * per_owner : (j + 1) * per_owner], pushed)
        to_hist[k][:, cap : cap + per_owner] = pushed


def pick(held, asked, slot, rows):
    wanted = asked[:, slot * 128 : slot * 128 + 1]
    block = held[:rows, :]
    for j in range(1, held.shape[0] // rows):
        block = jnp.where(
            jnp.broadcast_to(wanted == j, block.shape), held[j * rows : (j + 1) * rows, :], block
        )
    return block


def one_hop(k):
    return k > 1 and k & (k - 1) == 0


def pick_own_kernel(hidden, *refs):
    asked, outs = refs[: len(refs) // 2], refs[len(refs) // 2 :]
    for one, out in zip(asked, outs):
        out[...] = pick(hidden, one, 1, out.shape[0])


def pick_far_kernel(rows, hidden, far, *refs):
    asked, outs = refs[: len(refs) // 2], refs[len(refs) // 2 :]
    for one, out in zip(asked, outs):
        out[:rows, :] = pick(far, one, 0, rows)
        if out.shape[0] > rows:
            out[rows:, :] = pick(hidden, one, 1, rows)


def spread_kernel(per_dev, place, src, dst, tiles, out):
    block = tiles.shape[1]
    out[...] = jnp.zeros_like(out)
    for t in range(tiles.shape[0]):
        rows = pl.ds(pl.multiple_of(dst[0, t] * block, block), block)
        out[(src[0, t] // per_dev) ^ place[0], rows, :] = tiles[t]


def load_kernel(history, after, out):
    out[...] = history[...]


def pull_kernel(n_hist, cap, history, *refs):
    asked, outs = refs[:n_hist], refs[n_hist:]
    held = lax.broadcasted_iota(jnp.int32, (history.shape[0], cap), 0)
    for k in range(n_hist):
        hot = jnp.where(held == asked[k][:, :cap], 1.0, 0.0).astype(jnp.bfloat16)
        outs[k][...] = lax.dot_general(
            hot, history[...], (((0,), (0,)), ((), ())), preferred_element_type=jnp.float32
        ).astype(jnp.bfloat16)


def prepare_kernel(n_hist, cap, history, *refs):
    asked, sent = refs[:n_hist], refs[n_hist : 2 * n_hist]
    base, hot, refreshed, index, sem = refs[2 * n_hist :]
    h = lax.axis_index("hist")
    size = index.shape[1] // n_hist
    copies = []
    for k in range(n_hist):
        to = refreshed.at[pl.ds(pl.multiple_of((h ^ k) * size, size), size), :]
        copies.append(pltpu.make_async_copy(sent[k], to, sem.at[k]))
        copies[-1].start()
        index[:, k * size : (k + 1) * size] = asked[k][:, cap : cap + size]
    held = lax.broadcasted_iota(jnp.int32, hot.shape, 0)
    found = jnp.where(held == index[...], 1.0, 0.0)
    hot[...] = found.astype(jnp.bfloat16)
    hit = jnp.sum(found, axis=1, keepdims=True)
    base[...] = jnp.where(hit > 0.0, 0.0, history[...].astype(jnp.float32)).astype(jnp.bfloat16)
    for copy in copies:
        copy.wait()


def partial_kernel(n_hist, n_half, cap, own_adj, hidden, pull_adj, initial, spread, mine, *refs):
    arrived, early, out = refs[:n_hist], refs[n_hist:-1], refs[-1]
    h = lax.axis_index("hist")
    total = jnp.dot(own_adj[...], hidden[...], preferred_element_type=jnp.float32)
    total += jnp.dot(spread[n_half], mine[...], preferred_element_type=jnp.float32)
    for k, one in zip([k for k in range(n_half) if k and one_hop(k)], early):
        total += jnp.dot(spread[k], one[...], preferred_element_type=jnp.float32)
    for k in range(n_hist):
        columns = pl.ds(pl.multiple_of((h ^ k) * cap, cap), cap)
        total += jnp.dot(pull_adj[:, columns], arrived[k][...], preferred_element_type=jnp.float32)
    out[...] = (1.0 - alpha_init) * total + alpha_init * initial[...].astype(jnp.float32)


def final_kernel(n_half, chunks, first, part, spread, weight, *refs):
    late, sent, total, support = refs[: n_half - 1], refs[n_half - 1 : -2], refs[-2], refs[-1]
    block = spread.shape[2]
    size = sent[0].shape[0]
    for i, k in enumerate(chunks):
        rows = pl.ds(pl.multiple_of((lax.axis_index("hist") ^ k) * size, size), size)
        here = slice(i * size, (i + 1) * size)
        total[here, :] = part[rows, :]
        for j in range(1, n_half):
            total[here, :] += (1.0 - alpha_init) * jnp.dot(
                spread[n_half + j, rows, :], late[j - 1][:block, :], preferred_element_type=jnp.float32
            )
            if not one_hop(j):
                total[here, :] += (1.0 - alpha_init) * jnp.dot(
                    spread[j, rows, :], late[j - 1][block:, :], preferred_element_type=jnp.float32
                )
    support[...] = total[...].astype(jnp.bfloat16)
    projected = jnp.dot(support[...], weight[...], preferred_element_type=jnp.float32)
    result = jnp.maximum(
        (1.0 - beta_map) * support[...].astype(jnp.float32) + beta_map * projected, 0.0
    ).astype(jnp.bfloat16)
    for i in range(len(chunks)):
        sent[i][...] = result[i * size : (i + 1) * size, :]


def scatter_kernel(steps, base, hot, *refs):
    pushed, (out, rows, new, sem) = refs[:-4], refs[-4:]
    size = pushed[0].shape[0]
    for k, one in enumerate(pushed):
        rows[k * size : (k + 1) * size, :] = one[...]
    step = base.shape[0] // steps
    copies = []
    for i in range(steps):
        at = slice(i * step, (i + 1) * step)
        found = jnp.dot(hot[at, :], rows[...], preferred_element_type=jnp.float32)
        new[at, :] = (base[at, :].astype(jnp.float32) + found).astype(jnp.bfloat16)
        copies.append(pltpu.make_async_copy(new.at[at, :], out.at[at, :], sem.at[i]))
        copies[-1].start()
    for copy in copies:
        copy.wait()


def local(
    hidden,
    initial,
    own_adj,
    tiles,
    tile_src,
    tile_dst,
    history,
    pull_rows,
    pull_count,
    pull_adj,
    weight,
    push_rows,
):
    rows_dev, feature = hidden.shape
    block_rows = tiles.shape[1]
    per_dev = rows_dev // block_rows
    n_blk = lax.axis_size("blk")
    n_hist = lax.axis_size("hist")
    cap = pull_rows.shape[2]
    per_owner = rows_dev // n_hist
    held = history.shape[0]
    n_half = n_blk // 2
    place = jnp.stack([lax.axis_index("blk"), lax.axis_index("hist")]).astype(jnp.int32)
    anywhere = pl.BlockSpec(memory_space=pl.ANY)

    def shape(s, dtype=jnp.bfloat16):
        return jax.ShapeDtypeStruct(s, dtype)

    far = swap(hidden, "blk", n_blk, n_half)
    asks = pl.pallas_call(
        functools.partial(message_kernel, n_hist, n_half, per_dev),
        out_shape=[shape((1, cap + 128), jnp.int32)] * n_hist
        + [shape((1, 256), jnp.int32) for k in range(n_half)],
        in_specs=[smem(), smem(), smem(), vmem(), vmem()],
        out_specs=[vmem()] * (n_hist + n_half),
        compiler_params=params(),
        name="message",
    )(place, tile_src, pull_count, pull_rows, push_rows.reshape(1, rows_dev))
    wanted = [asks[n_hist]] + [swap(asks[n_hist + k], "blk", n_blk, k) for k in range(1, n_half)]
    asked = [asks[0]] + [swap(asks[k], "hist", n_hist, k) for k in range(1, n_hist)]
    spread = pl.pallas_call(
        functools.partial(spread_kernel, per_dev),
        out_shape=shape((n_blk, rows_dev, block_rows)),
        in_specs=[smem()] * 3 + [vmem()],
        out_specs=vmem(),
        compiler_params=params(),
        cost_estimate=cost(0, n_blk * rows_dev * block_rows * 2),
        name="spread",
    )(place, tile_src, tile_dst, tiles)

    history = pl.pallas_call(
        load_kernel,
        out_shape=shape(history.shape),
        in_specs=[vmem(), anywhere],
        out_specs=vmem(),
        compiler_params=params(),
        cost_estimate=cost(0, held * feature * 4),
        name="load",
    )(history, spread)
    asked, wanted, history = lax.optimization_barrier((asked, wanted, history))

    fetched = pl.pallas_call(
        functools.partial(pull_kernel, n_hist, cap),
        out_shape=[shape((cap, feature))] * n_hist,
        in_specs=[vmem()] * (1 + n_hist),
        out_specs=[vmem()] * n_hist,
        compiler_params=params(),
        cost_estimate=cost(2 * n_hist * cap * held * feature, held * feature * 4),
        name="pull",
    )(history, *asked)
    arrived = [fetched[0]] + [swap(fetched[k], "hist", n_hist, k) for k in range(1, n_hist)]

    peers = range(1, n_half)
    soon = [k for k in peers if one_hop(k)]
    picked = pl.pallas_call(
        pick_own_kernel,
        out_shape=[shape((block_rows, feature))] * len(soon),
        in_specs=[vmem()] * (1 + len(soon)),
        out_specs=[vmem()] * len(soon),
        compiler_params=params(),
        cost_estimate=cost(0, n_half * 4 * block_rows * feature),
        name="pick_own",
    )(hidden, *[wanted[k] for k in soon])
    early = [swap(one, "blk", n_blk, k) for one, k in zip(picked, soon)]

    picked = pl.pallas_call(
        functools.partial(pick_far_kernel, block_rows),
        out_shape=[
            shape((2 * block_rows if k and not one_hop(k) else block_rows, feature))
            for k in range(n_half)
        ],
        in_specs=[vmem()] * (n_half + 2),
        out_specs=[vmem()] * n_half,
        compiler_params=params(),
        cost_estimate=cost(0, n_half * 4 * block_rows * feature),
        name="pick_far",
    )(hidden, far, *wanted)
    mine = picked[0]
    late = [swap(picked[k], "blk", n_blk, k) for k in peers]

    part = pl.pallas_call(
        functools.partial(partial_kernel, n_hist, n_half, cap),
        out_shape=shape((rows_dev, feature), jnp.float32),
        in_specs=[vmem()] * (6 + n_hist + len(early)),
        out_specs=vmem(),
        compiler_params=params(),
        cost_estimate=cost(2 * rows_dev * feature * (rows_dev + n_hist * cap), rows_dev * feature * 12),
        name="partial",
    )(own_adj, hidden, pull_adj, initial, spread, mine, *arrived, *early)

    def final(chunks, name, first):
        rows = len(chunks) * per_owner
        return pl.pallas_call(
            functools.partial(final_kernel, n_half, chunks),
            out_shape=[shape((per_owner, feature))] * len(chunks),
            in_specs=[anywhere] + [vmem()] * (2 + n_half),
            out_specs=[vmem()] * len(chunks),
            scratch_shapes=[VMEM((rows, feature), jnp.float32), VMEM((rows, feature), jnp.bfloat16)],
            compiler_params=params(),
            cost_estimate=cost(2 * rows * feature * feature, rows * feature * 12),
            name=name,
        )(first, part, spread, weight, *late)

    outer = final(list(range(2, n_hist)), "final_outer", mine)
    inner = final([0, 1], "final_inner", outer[0])
    sent = inner + outer
    pushed = [sent[0]] + [swap(sent[k], "hist", n_hist, k) for k in range(1, n_hist)]

    base, hot, refreshed = pl.pallas_call(
        functools.partial(prepare_kernel, n_hist, cap),
        out_shape=[shape((held, feature)), shape((held, rows_dev)), shape((rows_dev, feature))],
        in_specs=[vmem()] * (1 + 2 * n_hist),
        out_specs=[vmem(), vmem(), anywhere],
        scratch_shapes=[VMEM((1, rows_dev), jnp.int32), pltpu.SemaphoreType.DMA((n_hist,))],
        compiler_params=params(),
        cost_estimate=cost(held * rows_dev * 8, held * feature * 6),
        name="prepare",
    )(history, *asked, *sent)

    steps = 4
    new_history = pl.pallas_call(
        functools.partial(scatter_kernel, steps),
        out_shape=shape((held, feature)),
        in_specs=[vmem()] * (2 + n_hist),
        out_specs=anywhere,
        scratch_shapes=[
            VMEM((rows_dev, feature), jnp.bfloat16),
            VMEM((held, feature), jnp.bfloat16),
            pltpu.SemaphoreType.DMA((steps,)),
        ],
        compiler_params=params(),
        name="scatter",
    )(base, hot, *pushed)
    return (refreshed, new_history)


def solution(mesh):
    both = P(("blk", "hist"))
    return jax.shard_map(
        local,
        mesh=mesh,
        in_specs=(both,) * 10 + (P(), both),
        out_specs=(both, both),
        check_vma=False,
    )
```

```python
import functools

import jax
import jax.numpy as jnp
from jax import lax
from jax.experimental import pallas as pl
from jax.experimental.pallas import tpu as pltpu
from jax.sharding import PartitionSpec as P

alpha_init = 0.1
beta_map = 0.4

VMEM = pltpu.VMEM
SMEM = pltpu.SMEM
LIMIT = 24 * 1024 * 1024


def vmem():
    return pl.BlockSpec(memory_space=VMEM)


def smem():
    return pl.BlockSpec(memory_space=SMEM)


def cost(flops, size):
    return pl.CostEstimate(flops=flops, bytes_accessed=size, transcendentals=0)


def params():
    return pltpu.CompilerParams(vmem_limit_bytes=LIMIT)


def swap(x, axis, n, k):
    return lax.ppermute(x, axis, [(i, i ^ k) for i in range(n)])


def message_kernel(n_hist, n_half, per_dev, place, src, count, rows, push, *outs):
    to_hist, to_half = outs[:n_hist], outs[n_hist:]
    cap = rows.shape[2]
    per_owner = push.shape[1] // n_hist
    b, h = place[0], place[1]
    for k in range(n_half):
        for slot, name in enumerate((k + n_half, k)):
            wanted = 0
            for t in range(src.shape[1]):
                wanted = jnp.where((src[0, t] // per_dev) ^ b == name, src[0, t] % per_dev, wanted)
            to_half[k][:, slot * 128 : slot * 128 + 128] = jnp.full((1, 128), wanted, jnp.int32)
    lane = lax.broadcasted_iota(jnp.int32, (1, cap), 1)
    for k in range(n_hist):
        o = h ^ k
        to_hist[k][:, :cap] = jnp.where(lane < count[0, o], rows[0, pl.ds(o, 1), :], -1)
        pushed = push[:, :per_owner]
        for j in range(1, n_hist):
            pushed = jnp.where(o == j, push[:, j * per_owner : (j + 1) * per_owner], pushed)
        to_hist[k][:, cap : cap + per_owner] = pushed


def pick(held, asked, slot, rows):
    wanted = asked[:, slot * 128 : slot * 128 + 1]
    block = held[:rows, :]
    for j in range(1, held.shape[0] // rows):
        block = jnp.where(
            jnp.broadcast_to(wanted == j, block.shape), held[j * rows : (j + 1) * rows, :], block
        )
    return block


def one_hop(k):
    return k > 1 and k & (k - 1) == 0


def pick_own_kernel(hidden, *refs):
    asked, outs = refs[: len(refs) // 2], refs[len(refs) // 2 :]
    for one, out in zip(asked, outs):
        out[...] = pick(hidden, one, 1, out.shape[0])


def pick_far_kernel(rows, hidden, far, after, *refs):
    asked, outs = refs[: len(refs) // 2], refs[len(refs) // 2 :]
    for one, out in zip(asked, outs):
        out[:rows, :] = pick(far, one, 0, rows)
        if out.shape[0] > rows:
            out[rows:, :] = pick(hidden, one, 1, rows)


def spread_kernel(per_dev, place, src, dst, tiles, out):
    block = tiles.shape[1]
    out[...] = jnp.zeros_like(out)
    for t in range(tiles.shape[0]):
        rows = pl.ds(pl.multiple_of(dst[0, t] * block, block), block)
        out[(src[0, t] // per_dev) ^ place[0], rows, :] = tiles[t]


def load_kernel(history, after, out):
    out[...] = history[...]


def pull_kernel(n_hist, cap, history, *refs):
    asked, outs = refs[:n_hist], refs[n_hist:]
    held = lax.broadcasted_iota(jnp.int32, (history.shape[0], cap), 0)
    for k in range(n_hist):
        hot = jnp.where(held == asked[k][:, :cap], 1.0, 0.0).astype(jnp.bfloat16)
        outs[k][...] = lax.dot_general(
            hot, history[...], (((0,), (0,)), ((), ())), preferred_element_type=jnp.float32
        ).astype(jnp.bfloat16)


def prepare_kernel(n_hist, cap, history, *refs):
    asked, sent = refs[:n_hist], refs[n_hist : 2 * n_hist]
    base, hot, refreshed, index, sem = refs[2 * n_hist :]
    h = lax.axis_index("hist")
    size = index.shape[1] // n_hist
    copies = []
    for k in range(n_hist):
        to = refreshed.at[pl.ds(pl.multiple_of((h ^ k) * size, size), size), :]
        copies.append(pltpu.make_async_copy(sent[k], to, sem.at[k]))
        copies[-1].start()
        index[:, k * size : (k + 1) * size] = asked[k][:, cap : cap + size]
    held = lax.broadcasted_iota(jnp.int32, hot.shape, 0)
    found = jnp.where(held == index[...], 1.0, 0.0)
    hot[...] = found.astype(jnp.bfloat16)
    hit = jnp.sum(found, axis=1, keepdims=True)
    base[...] = jnp.where(hit > 0.0, 0.0, history[...].astype(jnp.float32)).astype(jnp.bfloat16)
    for copy in copies:
        copy.wait()


def partial_kernel(n_hist, n_half, cap, own_adj, hidden, pull_adj, initial, spread, mine, *refs):
    arrived, early, out = refs[:n_hist], refs[n_hist:-1], refs[-1]
    h = lax.axis_index("hist")
    total = jnp.dot(own_adj[...], hidden[...], preferred_element_type=jnp.float32)
    total += jnp.dot(spread[n_half], mine[...], preferred_element_type=jnp.float32)
    for k, one in zip([k for k in range(n_half) if k and one_hop(k)], early):
        total += jnp.dot(spread[k], one[...], preferred_element_type=jnp.float32)
    for k in range(n_hist):
        columns = pl.ds(pl.multiple_of((h ^ k) * cap, cap), cap)
        total += jnp.dot(pull_adj[:, columns], arrived[k][...], preferred_element_type=jnp.float32)
    out[...] = (1.0 - alpha_init) * total + alpha_init * initial[...].astype(jnp.float32)


def final_kernel(n_half, chunks, first, part, spread, weight, *refs):
    late, sent, total, support = refs[: n_half - 1], refs[n_half - 1 : -2], refs[-2], refs[-1]
    block = spread.shape[2]
    size = sent[0].shape[0]
    for i, k in enumerate(chunks):
        rows = pl.ds(pl.multiple_of((lax.axis_index("hist") ^ k) * size, size), size)
        here = slice(i * size, (i + 1) * size)
        total[here, :] = part[rows, :]
        for j in range(1, n_half):
            total[here, :] += (1.0 - alpha_init) * jnp.dot(
                spread[n_half + j, rows, :], late[j - 1][:block, :], preferred_element_type=jnp.float32
            )
            if not one_hop(j):
                total[here, :] += (1.0 - alpha_init) * jnp.dot(
                    spread[j, rows, :], late[j - 1][block:, :], preferred_element_type=jnp.float32
                )
    support[...] = total[...].astype(jnp.bfloat16)
    projected = jnp.dot(support[...], weight[...], preferred_element_type=jnp.float32)
    result = jnp.maximum(
        (1.0 - beta_map) * support[...].astype(jnp.float32) + beta_map * projected, 0.0
    ).astype(jnp.bfloat16)
    for i in range(len(chunks)):
        sent[i][...] = result[i * size : (i + 1) * size, :]


def scatter_kernel(steps, base, hot, *refs):
    pushed, (out, rows, new, sem) = refs[:-4], refs[-4:]
    size = pushed[0].shape[0]
    for k, one in enumerate(pushed):
        rows[k * size : (k + 1) * size, :] = one[...]
    step = base.shape[0] // steps
    copies = []
    for i in range(steps):
        at = slice(i * step, (i + 1) * step)
        found = jnp.dot(hot[at, :], rows[...], preferred_element_type=jnp.float32)
        new[at, :] = (base[at, :].astype(jnp.float32) + found).astype(jnp.bfloat16)
        copies.append(pltpu.make_async_copy(new.at[at, :], out.at[at, :], sem.at[i]))
        copies[-1].start()
    for copy in copies:
        copy.wait()


def local(
    hidden,
    initial,
    own_adj,
    tiles,
    tile_src,
    tile_dst,
    history,
    pull_rows,
    pull_count,
    pull_adj,
    weight,
    push_rows,
):
    rows_dev, feature = hidden.shape
    block_rows = tiles.shape[1]
    per_dev = rows_dev // block_rows
    n_blk = lax.axis_size("blk")
    n_hist = lax.axis_size("hist")
    cap = pull_rows.shape[2]
    per_owner = rows_dev // n_hist
    held = history.shape[0]
    n_half = n_blk // 2
    place = jnp.stack([lax.axis_index("blk"), lax.axis_index("hist")]).astype(jnp.int32)
    anywhere = pl.BlockSpec(memory_space=pl.ANY)

    def shape(s, dtype=jnp.bfloat16):
        return jax.ShapeDtypeStruct(s, dtype)

    far = swap(hidden, "blk", n_blk, n_half)
    asks = pl.pallas_call(
        functools.partial(message_kernel, n_hist, n_half, per_dev),
        out_shape=[shape((1, cap + 128), jnp.int32)] * n_hist
        + [shape((1, 256), jnp.int32) for k in range(n_half)],
        in_specs=[smem(), smem(), smem(), vmem(), vmem()],
        out_specs=[vmem()] * (n_hist + n_half),
        compiler_params=params(),
        name="message",
    )(place, tile_src, pull_count, pull_rows, push_rows.reshape(1, rows_dev))
    wanted = [asks[n_hist]] + [swap(asks[n_hist + k], "blk", n_blk, k) for k in range(1, n_half)]
    asked = [asks[0]] + [swap(asks[k], "hist", n_hist, k) for k in range(1, n_hist)]
    spread = pl.pallas_call(
        functools.partial(spread_kernel, per_dev),
        out_shape=shape((n_blk, rows_dev, block_rows)),
        in_specs=[smem()] * 3 + [vmem()],
        out_specs=vmem(),
        compiler_params=params(),
        cost_estimate=cost(0, n_blk * rows_dev * block_rows * 2),
        name="spread",
    )(place, tile_src, tile_dst, tiles)

    history = pl.pallas_call(
        load_kernel,
        out_shape=shape(history.shape),
        in_specs=[vmem(), anywhere],
        out_specs=vmem(),
        compiler_params=params(),
        cost_estimate=cost(0, held * feature * 4),
        name="load",
    )(history, spread)
    asked, wanted, history = lax.optimization_barrier((asked, wanted, history))

    fetched = pl.pallas_call(
        functools.partial(pull_kernel, n_hist, cap),
        out_shape=[shape((cap, feature))] * n_hist,
        in_specs=[vmem()] * (1 + n_hist),
        out_specs=[vmem()] * n_hist,
        compiler_params=params(),
        cost_estimate=cost(2 * n_hist * cap * held * feature, held * feature * 4),
        name="pull",
    )(history, *asked)
    arrived = [fetched[0]] + [swap(fetched[k], "hist", n_hist, k) for k in range(1, n_hist)]

    peers = range(1, n_half)
    soon = [k for k in peers if one_hop(k)]
    picked = pl.pallas_call(
        pick_own_kernel,
        out_shape=[shape((block_rows, feature))] * len(soon),
        in_specs=[vmem()] * (1 + len(soon)),
        out_specs=[vmem()] * len(soon),
        compiler_params=params(),
        cost_estimate=cost(0, n_half * 4 * block_rows * feature),
        name="pick_own",
    )(hidden, *[wanted[k] for k in soon])
    early = [swap(one, "blk", n_blk, k) for one, k in zip(picked, soon)]

    picked = pl.pallas_call(
        functools.partial(pick_far_kernel, block_rows),
        out_shape=[
            shape((2 * block_rows if k and not one_hop(k) else block_rows, feature))
            for k in range(n_half)
        ],
        in_specs=[vmem(), vmem(), anywhere] + [vmem()] * n_half,
        out_specs=[vmem()] * n_half,
        compiler_params=params(),
        cost_estimate=cost(0, n_half * 4 * block_rows * feature),
        name="pick_far",
    )(hidden, far, arrived[1], *wanted)
    mine = picked[0]
    late = [swap(picked[k], "blk", n_blk, k) for k in peers]

    part = pl.pallas_call(
        functools.partial(partial_kernel, n_hist, n_half, cap),
        out_shape=shape((rows_dev, feature), jnp.float32),
        in_specs=[vmem()] * (6 + n_hist + len(early)),
        out_specs=vmem(),
        compiler_params=params(),
        cost_estimate=cost(2 * rows_dev * feature * (rows_dev + n_hist * cap), rows_dev * feature * 12),
        name="partial",
    )(own_adj, hidden, pull_adj, initial, spread, mine, *arrived, *early)

    def final(chunks, name, first):
        rows = len(chunks) * per_owner
        return pl.pallas_call(
            functools.partial(final_kernel, n_half, chunks),
            out_shape=[shape((per_owner, feature))] * len(chunks),
            in_specs=[anywhere] + [vmem()] * (2 + n_half),
            out_specs=[vmem()] * len(chunks),
            scratch_shapes=[VMEM((rows, feature), jnp.float32), VMEM((rows, feature), jnp.bfloat16)],
            compiler_params=params(),
            cost_estimate=cost(2 * rows * feature * feature, rows * feature * 12),
            name=name,
        )(first, part, spread, weight, *late)

    outer = final(list(range(1, n_hist)), "final_sent", mine)
    inner = final([0], "final_kept", outer[0])
    sent = inner + outer
    pushed = [sent[0]] + [swap(sent[k], "hist", n_hist, k) for k in range(1, n_hist)]

    base, hot, refreshed = pl.pallas_call(
        functools.partial(prepare_kernel, n_hist, cap),
        out_shape=[shape((held, feature)), shape((held, rows_dev)), shape((rows_dev, feature))],
        in_specs=[vmem()] * (1 + 2 * n_hist),
        out_specs=[vmem(), vmem(), anywhere],
        scratch_shapes=[VMEM((1, rows_dev), jnp.int32), pltpu.SemaphoreType.DMA((n_hist,))],
        compiler_params=params(),
        cost_estimate=cost(held * rows_dev * 8, held * feature * 6),
        name="prepare",
    )(history, *asked, *sent)

    steps = 4
    new_history = pl.pallas_call(
        functools.partial(scatter_kernel, steps),
        out_shape=shape((held, feature)),
        in_specs=[vmem()] * (2 + n_hist),
        out_specs=anywhere,
        scratch_shapes=[
            VMEM((rows_dev, feature), jnp.bfloat16),
            VMEM((held, feature), jnp.bfloat16),
            pltpu.SemaphoreType.DMA((steps,)),
        ],
        compiler_params=params(),
        name="scatter",
    )(base, hot, *pushed)
    return (refreshed, new_history)


def solution(mesh):
    both = P(("blk", "hist"))
    return jax.shard_map(
        local,
        mesh=mesh,
        in_specs=(both,) * 10 + (P(), both),
        out_specs=(both, both),
        check_vma=False,
    )
```

```python
import functools

import jax
import jax.numpy as jnp
from jax import lax
from jax.experimental import pallas as pl
from jax.experimental.pallas import tpu as pltpu
from jax.sharding import PartitionSpec as P

alpha_init = 0.1
beta_map = 0.4

VMEM = pltpu.VMEM
SMEM = pltpu.SMEM
LIMIT = 24 * 1024 * 1024


def vmem():
    return pl.BlockSpec(memory_space=VMEM)


def smem():
    return pl.BlockSpec(memory_space=SMEM)


def cost(flops, size):
    return pl.CostEstimate(flops=flops, bytes_accessed=size, transcendentals=0)


def params():
    return pltpu.CompilerParams(vmem_limit_bytes=LIMIT)


def swap(x, axis, n, k):
    return lax.ppermute(x, axis, [(i, i ^ k) for i in range(n)])


def message_kernel(n_hist, n_half, per_dev, after, src, count, rows, push, *outs):
    to_hist, to_half = outs[:n_hist], outs[n_hist:]
    cap = rows.shape[2]
    per_owner = push.shape[1] // n_hist
    b, h = lax.axis_index("blk"), lax.axis_index("hist")
    name = lax.div(src[...], per_dev) ^ b
    local = lax.rem(src[...], per_dev)
    for k in range(n_half):
        for slot, wanted in enumerate((k + n_half, k)):
            found = jnp.sum(jnp.where(name == wanted, local, 0), axis=1, keepdims=True)
            to_half[k][:, slot * 128 : slot * 128 + 128] = jnp.broadcast_to(found, (1, 128))
    owner = lax.broadcasted_iota(jnp.int32, count.shape, 1)
    lane = lax.broadcasted_iota(jnp.int32, (1, cap), 1)
    for k in range(n_hist):
        o = h ^ k
        used = jnp.sum(jnp.where(owner == o, count[...], 0), axis=1, keepdims=True)
        to_hist[k][:, :cap] = jnp.where(lane < used, rows[0, pl.ds(o, 1), :], -1)
        pushed = push[:, :per_owner]
        for j in range(1, n_hist):
            pushed = jnp.where(o == j, push[:, j * per_owner : (j + 1) * per_owner], pushed)
        to_hist[k][:, cap : cap + per_owner] = pushed


def pick(held, asked, slot, rows):
    wanted = asked[:, slot * 128 : slot * 128 + 1]
    block = held[:rows, :]
    for j in range(1, held.shape[0] // rows):
        block = jnp.where(
            jnp.broadcast_to(wanted == j, block.shape), held[j * rows : (j + 1) * rows, :], block
        )
    return block


def one_hop(k):
    return k > 1 and k & (k - 1) == 0


def pick_own_kernel(hidden, *refs):
    asked, outs = refs[: len(refs) // 2], refs[len(refs) // 2 :]
    for one, out in zip(asked, outs):
        out[...] = pick(hidden, one, 1, out.shape[0])


def pick_far_kernel(rows, hidden, far, after, *refs):
    asked, outs = refs[: len(refs) // 2], refs[len(refs) // 2 :]
    for one, out in zip(asked, outs):
        out[:rows, :] = pick(far, one, 0, rows)
        if out.shape[0] > rows:
            out[rows:, :] = pick(hidden, one, 1, rows)


def spread_kernel(per_dev, place, src, dst, tiles, out):
    block = tiles.shape[1]
    out[...] = jnp.zeros_like(out)
    for t in range(tiles.shape[0]):
        rows = pl.ds(pl.multiple_of(dst[0, t] * block, block), block)
        out[(src[0, t] // per_dev) ^ place[0], rows, :] = tiles[t]


def load_kernel(history, after, out):
    out[...] = history[...]


def pull_kernel(n_hist, cap, history, *refs):
    asked, outs = refs[:n_hist], refs[n_hist:]
    held = lax.broadcasted_iota(jnp.int32, (history.shape[0], cap), 0)
    for k in range(n_hist):
        hot = jnp.where(held == asked[k][:, :cap], 1.0, 0.0).astype(jnp.bfloat16)
        outs[k][...] = lax.dot_general(
            hot, history[...], (((0,), (0,)), ((), ())), preferred_element_type=jnp.float32
        ).astype(jnp.bfloat16)


def prepare_kernel(n_hist, cap, history, *refs):
    asked, sent = refs[:n_hist], refs[n_hist : 2 * n_hist]
    base, hot, refreshed, index, sem = refs[2 * n_hist :]
    h = lax.axis_index("hist")
    size = index.shape[1] // n_hist
    copies = []
    for k in range(n_hist):
        to = refreshed.at[pl.ds(pl.multiple_of((h ^ k) * size, size), size), :]
        copies.append(pltpu.make_async_copy(sent[k], to, sem.at[k]))
        copies[-1].start()
        index[:, k * size : (k + 1) * size] = asked[k][:, cap : cap + size]
    held = lax.broadcasted_iota(jnp.int32, hot.shape, 0)
    found = jnp.where(held == index[...], 1.0, 0.0)
    hot[...] = found.astype(jnp.bfloat16)
    hit = jnp.sum(found, axis=1, keepdims=True)
    base[...] = jnp.where(hit > 0.0, 0.0, history[...].astype(jnp.float32)).astype(jnp.bfloat16)
    for copy in copies:
        copy.wait()


def partial_kernel(n_hist, n_half, cap, own_adj, hidden, pull_adj, initial, spread, mine, *refs):
    arrived, early, out = refs[:n_hist], refs[n_hist:-1], refs[-1]
    h = lax.axis_index("hist")
    total = jnp.dot(own_adj[...], hidden[...], preferred_element_type=jnp.float32)
    total += jnp.dot(spread[n_half], mine[...], preferred_element_type=jnp.float32)
    for k, one in zip([k for k in range(n_half) if k and one_hop(k)], early):
        total += jnp.dot(spread[k], one[...], preferred_element_type=jnp.float32)
    for k in range(n_hist):
        columns = pl.ds(pl.multiple_of((h ^ k) * cap, cap), cap)
        total += jnp.dot(pull_adj[:, columns], arrived[k][...], preferred_element_type=jnp.float32)
    out[...] = (1.0 - alpha_init) * total + alpha_init * initial[...].astype(jnp.float32)


def final_kernel(n_half, chunks, first, part, spread, weight, *refs):
    late, sent, total, support = refs[: n_half - 1], refs[n_half - 1 : -2], refs[-2], refs[-1]
    block = spread.shape[2]
    size = sent[0].shape[0]
    for i, k in enumerate(chunks):
        rows = pl.ds(pl.multiple_of((lax.axis_index("hist") ^ k) * size, size), size)
        here = slice(i * size, (i + 1) * size)
        total[here, :] = part[rows, :]
        for j in range(1, n_half):
            total[here, :] += (1.0 - alpha_init) * jnp.dot(
                spread[n_half + j, rows, :], late[j - 1][:block, :], preferred_element_type=jnp.float32
            )
            if not one_hop(j):
                total[here, :] += (1.0 - alpha_init) * jnp.dot(
                    spread[j, rows, :], late[j - 1][block:, :], preferred_element_type=jnp.float32
                )
    support[...] = total[...].astype(jnp.bfloat16)
    projected = jnp.dot(support[...], weight[...], preferred_element_type=jnp.float32)
    result = jnp.maximum(
        (1.0 - beta_map) * support[...].astype(jnp.float32) + beta_map * projected, 0.0
    ).astype(jnp.bfloat16)
    for i in range(len(chunks)):
        sent[i][...] = result[i * size : (i + 1) * size, :]


def scatter_kernel(steps, base, hot, *refs):
    pushed, (out, rows, new, sem) = refs[:-4], refs[-4:]
    size = pushed[0].shape[0]
    for k, one in enumerate(pushed):
        rows[k * size : (k + 1) * size, :] = one[...]
    step = base.shape[0] // steps
    copies = []
    for i in range(steps):
        at = slice(i * step, (i + 1) * step)
        found = jnp.dot(hot[at, :], rows[...], preferred_element_type=jnp.float32)
        new[at, :] = (base[at, :].astype(jnp.float32) + found).astype(jnp.bfloat16)
        copies.append(pltpu.make_async_copy(new.at[at, :], out.at[at, :], sem.at[i]))
        copies[-1].start()
    for copy in copies:
        copy.wait()


def local(
    hidden,
    initial,
    own_adj,
    tiles,
    tile_src,
    tile_dst,
    history,
    pull_rows,
    pull_count,
    pull_adj,
    weight,
    push_rows,
):
    rows_dev, feature = hidden.shape
    block_rows = tiles.shape[1]
    per_dev = rows_dev // block_rows
    n_blk = lax.axis_size("blk")
    n_hist = lax.axis_size("hist")
    cap = pull_rows.shape[2]
    per_owner = rows_dev // n_hist
    held = history.shape[0]
    n_half = n_blk // 2
    place = jnp.stack([lax.axis_index("blk"), lax.axis_index("hist")]).astype(jnp.int32)
    anywhere = pl.BlockSpec(memory_space=pl.ANY)

    def shape(s, dtype=jnp.bfloat16):
        return jax.ShapeDtypeStruct(s, dtype)

    far = swap(hidden, "blk", n_blk, n_half)
    asks = pl.pallas_call(
        functools.partial(message_kernel, n_hist, n_half, per_dev),
        out_shape=[shape((1, cap + 128), jnp.int32)] * n_hist
        + [shape((1, 256), jnp.int32) for k in range(n_half)],
        in_specs=[anywhere] + [vmem()] * 4,
        out_specs=[vmem()] * (n_hist + n_half),
        compiler_params=params(),
        name="message",
    )(place, tile_src, pull_count, pull_rows, push_rows.reshape(1, rows_dev))
    wanted = [asks[n_hist]] + [swap(asks[n_hist + k], "blk", n_blk, k) for k in range(1, n_half)]
    asked = [asks[0]] + [swap(asks[k], "hist", n_hist, k) for k in range(1, n_hist)]
    spread = pl.pallas_call(
        functools.partial(spread_kernel, per_dev),
        out_shape=shape((n_blk, rows_dev, block_rows)),
        in_specs=[smem()] * 3 + [vmem()],
        out_specs=vmem(),
        compiler_params=params(),
        cost_estimate=cost(0, n_blk * rows_dev * block_rows * 2),
        name="spread",
    )(place, tile_src, tile_dst, tiles)

    history = pl.pallas_call(
        load_kernel,
        out_shape=shape(history.shape),
        in_specs=[vmem(), anywhere],
        out_specs=vmem(),
        compiler_params=params(),
        cost_estimate=cost(0, held * feature * 4),
        name="load",
    )(history, spread)
    asked, wanted, history = lax.optimization_barrier((asked, wanted, history))

    fetched = pl.pallas_call(
        functools.partial(pull_kernel, n_hist, cap),
        out_shape=[shape((cap, feature))] * n_hist,
        in_specs=[vmem()] * (1 + n_hist),
        out_specs=[vmem()] * n_hist,
        compiler_params=params(),
        cost_estimate=cost(2 * n_hist * cap * held * feature, held * feature * 4),
        name="pull",
    )(history, *asked)
    arrived = [fetched[0]] + [swap(fetched[k], "hist", n_hist, k) for k in range(1, n_hist)]

    peers = range(1, n_half)
    soon = [k for k in peers if one_hop(k)]
    picked = pl.pallas_call(
        pick_own_kernel,
        out_shape=[shape((block_rows, feature))] * len(soon),
        in_specs=[vmem()] * (1 + len(soon)),
        out_specs=[vmem()] * len(soon),
        compiler_params=params(),
        cost_estimate=cost(0, n_half * 4 * block_rows * feature),
        name="pick_own",
    )(hidden, *[wanted[k] for k in soon])
    early = [swap(one, "blk", n_blk, k) for one, k in zip(picked, soon)]

    picked = pl.pallas_call(
        functools.partial(pick_far_kernel, block_rows),
        out_shape=[
            shape((2 * block_rows if k and not one_hop(k) else block_rows, feature))
            for k in range(n_half)
        ],
        in_specs=[vmem(), vmem(), anywhere] + [vmem()] * n_half,
        out_specs=[vmem()] * n_half,
        compiler_params=params(),
        cost_estimate=cost(0, n_half * 4 * block_rows * feature),
        name="pick_far",
    )(hidden, far, arrived[1], *wanted)
    mine = picked[0]
    late = [swap(picked[k], "blk", n_blk, k) for k in peers]

    part = pl.pallas_call(
        functools.partial(partial_kernel, n_hist, n_half, cap),
        out_shape=shape((rows_dev, feature), jnp.float32),
        in_specs=[vmem()] * (6 + n_hist + len(early)),
        out_specs=vmem(),
        compiler_params=params(),
        cost_estimate=cost(2 * rows_dev * feature * (rows_dev + n_hist * cap), rows_dev * feature * 12),
        name="partial",
    )(own_adj, hidden, pull_adj, initial, spread, mine, *arrived, *early)

    def final(chunks, name, first):
        rows = len(chunks) * per_owner
        return pl.pallas_call(
            functools.partial(final_kernel, n_half, chunks),
            out_shape=[shape((per_owner, feature))] * len(chunks),
            in_specs=[anywhere] + [vmem()] * (2 + n_half),
            out_specs=[vmem()] * len(chunks),
            scratch_shapes=[VMEM((rows, feature), jnp.float32), VMEM((rows, feature), jnp.bfloat16)],
            compiler_params=params(),
            cost_estimate=cost(2 * rows * feature * feature, rows * feature * 12),
            name=name,
        )(first, part, spread, weight, *late)

    outer = final(list(range(1, n_hist)), "final_sent", mine)
    inner = final([0], "final_kept", outer[0])
    sent = inner + outer
    pushed = [sent[0]] + [swap(sent[k], "hist", n_hist, k) for k in range(1, n_hist)]

    base, hot, refreshed = pl.pallas_call(
        functools.partial(prepare_kernel, n_hist, cap),
        out_shape=[shape((held, feature)), shape((held, rows_dev)), shape((rows_dev, feature))],
        in_specs=[vmem()] * (1 + 2 * n_hist),
        out_specs=[vmem(), vmem(), anywhere],
        scratch_shapes=[VMEM((1, rows_dev), jnp.int32), pltpu.SemaphoreType.DMA((n_hist,))],
        compiler_params=params(),
        cost_estimate=cost(held * rows_dev * 8, held * feature * 6),
        name="prepare",
    )(history, *asked, *sent)

    steps = 4
    new_history = pl.pallas_call(
        functools.partial(scatter_kernel, steps),
        out_shape=shape((held, feature)),
        in_specs=[vmem()] * (2 + n_hist),
        out_specs=anywhere,
        scratch_shapes=[
            VMEM((rows_dev, feature), jnp.bfloat16),
            VMEM((held, feature), jnp.bfloat16),
            pltpu.SemaphoreType.DMA((steps,)),
        ],
        compiler_params=params(),
        name="scatter",
    )(base, hot, *pushed)
    return (refreshed, new_history)


def solution(mesh):
    both = P(("blk", "hist"))
    return jax.shard_map(
        local,
        mesh=mesh,
        in_specs=(both,) * 10 + (P(), both),
        out_specs=(both, both),
        check_vma=False,
    )
```

```python
import functools

import jax
import jax.numpy as jnp
from jax import lax
from jax.experimental import pallas as pl
from jax.experimental.pallas import tpu as pltpu
from jax.sharding import PartitionSpec as P

alpha_init = 0.1
beta_map = 0.4

VMEM = pltpu.VMEM
SMEM = pltpu.SMEM
LIMIT = 24 * 1024 * 1024


def vmem():
    return pl.BlockSpec(memory_space=VMEM)


def smem():
    return pl.BlockSpec(memory_space=SMEM)


def cost(flops, size):
    return pl.CostEstimate(flops=flops, bytes_accessed=size, transcendentals=0)


def params():
    return pltpu.CompilerParams(vmem_limit_bytes=LIMIT)


def swap(x, axis, n, k):
    return lax.ppermute(x, axis, [(i, i ^ k) for i in range(n)])


def message_kernel(n_hist, n_half, per_dev, after, src, count, rows, push, *outs):
    to_hist, to_half = outs[:n_hist], outs[n_hist:]
    cap = rows.shape[2]
    per_owner = push.shape[1] // n_hist
    b, h = lax.axis_index("blk"), lax.axis_index("hist")
    name = lax.div(src[...], per_dev) ^ b
    local = lax.rem(src[...], per_dev)
    for k in range(n_half):
        for slot, wanted in enumerate((k + n_half, k)):
            found = jnp.sum(jnp.where(name == wanted, local, 0), axis=1, keepdims=True)
            to_half[k][:, slot * 128 : slot * 128 + 128] = jnp.broadcast_to(found, (1, 128))
    owner = lax.broadcasted_iota(jnp.int32, count.shape, 1)
    lane = lax.broadcasted_iota(jnp.int32, (1, cap), 1)
    for k in range(n_hist):
        o = h ^ k
        used = jnp.sum(jnp.where(owner == o, count[...], 0), axis=1, keepdims=True)
        to_hist[k][:, :cap] = jnp.where(lane < used, rows[0, pl.ds(o, 1), :], -1)
        pushed = push[:, :per_owner]
        for j in range(1, n_hist):
            pushed = jnp.where(o == j, push[:, j * per_owner : (j + 1) * per_owner], pushed)
        to_hist[k][:, cap : cap + per_owner] = pushed


def pick(held, asked, slot, rows):
    wanted = asked[:, slot * 128 : slot * 128 + 1]
    block = held[:rows, :]
    for j in range(1, held.shape[0] // rows):
        block = jnp.where(
            jnp.broadcast_to(wanted == j, block.shape), held[j * rows : (j + 1) * rows, :], block
        )
    return block


def one_hop(k):
    return k > 1 and k & (k - 1) == 0


def pick_own_kernel(hidden, *refs):
    asked, outs = refs[: len(refs) // 2], refs[len(refs) // 2 :]
    for one, out in zip(asked, outs):
        out[...] = pick(hidden, one, 1, out.shape[0])


def pick_far_kernel(rows, peers, hidden, far, after, *refs):
    asked, outs = refs[: len(peers)], refs[len(peers) :]
    for one, out in zip(asked, outs):
        out[:rows, :] = pick(far, one, 0, rows)
        if out.shape[0] > rows:
            out[rows:, :] = pick(hidden, one, 1, rows)


def spread_kernel(per_dev, place, src, dst, tiles, after, out):
    block = tiles.shape[1]
    out[...] = jnp.zeros_like(out)
    for t in range(tiles.shape[0]):
        rows = pl.ds(pl.multiple_of(dst[0, t] * block, block), block)
        out[(src[0, t] // per_dev) ^ place[0], rows, :] = tiles[t]


def load_kernel(history, out):
    out[...] = history[...]


def pull_kernel(n_hist, cap, history, *refs):
    asked, outs = refs[:n_hist], refs[n_hist:]
    held = lax.broadcasted_iota(jnp.int32, (history.shape[0], cap), 0)
    for k in range(n_hist):
        hot = jnp.where(held == asked[k][:, :cap], 1.0, 0.0).astype(jnp.bfloat16)
        outs[k][...] = lax.dot_general(
            hot, history[...], (((0,), (0,)), ((), ())), preferred_element_type=jnp.float32
        ).astype(jnp.bfloat16)


def prepare_kernel(n_hist, cap, history, *refs):
    asked, sent = refs[:n_hist], refs[n_hist : 2 * n_hist]
    base, hot, refreshed, index, sem = refs[2 * n_hist :]
    h = lax.axis_index("hist")
    size = index.shape[1] // n_hist
    copies = []
    for k in range(n_hist):
        to = refreshed.at[pl.ds(pl.multiple_of((h ^ k) * size, size), size), :]
        copies.append(pltpu.make_async_copy(sent[k], to, sem.at[k]))
        copies[-1].start()
        index[:, k * size : (k + 1) * size] = asked[k][:, cap : cap + size]
    held = lax.broadcasted_iota(jnp.int32, hot.shape, 0)
    found = jnp.where(held == index[...], 1.0, 0.0)
    hot[...] = found.astype(jnp.bfloat16)
    hit = jnp.sum(found, axis=1, keepdims=True)
    base[...] = jnp.where(hit > 0.0, 0.0, history[...].astype(jnp.float32)).astype(jnp.bfloat16)
    for copy in copies:
        copy.wait()


def partial_kernel(n_hist, n_half, cap, own_adj, hidden, pull_adj, initial, spread, mine, *refs):
    arrived, early, out = refs[:n_hist], refs[n_hist:-1], refs[-1]
    h = lax.axis_index("hist")
    total = jnp.dot(own_adj[...], hidden[...], preferred_element_type=jnp.float32)
    total += jnp.dot(spread[n_half], mine[...], preferred_element_type=jnp.float32)
    for k, one in zip([k for k in range(n_half) if k and one_hop(k)], early):
        total += jnp.dot(spread[k], one[...], preferred_element_type=jnp.float32)
    for k in range(n_hist):
        columns = pl.ds(pl.multiple_of((h ^ k) * cap, cap), cap)
        total += jnp.dot(pull_adj[:, columns], arrived[k][...], preferred_element_type=jnp.float32)
    out[...] = (1.0 - alpha_init) * total + alpha_init * initial[...].astype(jnp.float32)


def final_kernel(n_half, chunks, first, part, spread, weight, *refs):
    late, sent, total, support = refs[: n_half - 1], refs[n_half - 1 : -2], refs[-2], refs[-1]
    block = spread.shape[2]
    size = sent[0].shape[0]
    for i, k in enumerate(chunks):
        rows = pl.ds(pl.multiple_of((lax.axis_index("hist") ^ k) * size, size), size)
        here = slice(i * size, (i + 1) * size)
        total[here, :] = part[rows, :]
        for j in range(1, n_half):
            total[here, :] += (1.0 - alpha_init) * jnp.dot(
                spread[n_half + j, rows, :], late[j - 1][:block, :], preferred_element_type=jnp.float32
            )
            if not one_hop(j):
                total[here, :] += (1.0 - alpha_init) * jnp.dot(
                    spread[j, rows, :], late[j - 1][block:, :], preferred_element_type=jnp.float32
                )
    support[...] = total[...].astype(jnp.bfloat16)
    projected = jnp.dot(support[...], weight[...], preferred_element_type=jnp.float32)
    result = jnp.maximum(
        (1.0 - beta_map) * support[...].astype(jnp.float32) + beta_map * projected, 0.0
    ).astype(jnp.bfloat16)
    for i in range(len(chunks)):
        sent[i][...] = result[i * size : (i + 1) * size, :]


def scatter_kernel(steps, base, hot, *refs):
    pushed, (out, rows, new, sem) = refs[:-4], refs[-4:]
    size = pushed[0].shape[0]
    for k, one in enumerate(pushed):
        rows[k * size : (k + 1) * size, :] = one[...]
    step = base.shape[0] // steps
    copies = []
    for i in range(steps):
        at = slice(i * step, (i + 1) * step)
        found = jnp.dot(hot[at, :], rows[...], preferred_element_type=jnp.float32)
        new[at, :] = (base[at, :].astype(jnp.float32) + found).astype(jnp.bfloat16)
        copies.append(pltpu.make_async_copy(new.at[at, :], out.at[at, :], sem.at[i]))
        copies[-1].start()
    for copy in copies:
        copy.wait()


def local(
    hidden,
    initial,
    own_adj,
    tiles,
    tile_src,
    tile_dst,
    history,
    pull_rows,
    pull_count,
    pull_adj,
    weight,
    push_rows,
):
    rows_dev, feature = hidden.shape
    block_rows = tiles.shape[1]
    per_dev = rows_dev // block_rows
    n_blk = lax.axis_size("blk")
    n_hist = lax.axis_size("hist")
    cap = pull_rows.shape[2]
    per_owner = rows_dev // n_hist
    held = history.shape[0]
    n_half = n_blk // 2
    place = jnp.stack([lax.axis_index("blk"), lax.axis_index("hist")]).astype(jnp.int32)
    anywhere = pl.BlockSpec(memory_space=pl.ANY)

    def shape(s, dtype=jnp.bfloat16):
        return jax.ShapeDtypeStruct(s, dtype)

    far = swap(hidden, "blk", n_blk, n_half)
    asks = pl.pallas_call(
        functools.partial(message_kernel, n_hist, n_half, per_dev),
        out_shape=[shape((1, cap + 128), jnp.int32)] * n_hist
        + [shape((1, 256), jnp.int32) for k in range(n_half)],
        in_specs=[anywhere] + [vmem()] * 4,
        out_specs=[vmem()] * (n_hist + n_half),
        compiler_params=params(),
        name="message",
    )(place, tile_src, pull_count, pull_rows, push_rows.reshape(1, rows_dev))
    wanted = [asks[n_hist]] + [swap(asks[n_hist + k], "blk", n_blk, k) for k in range(1, n_half)]
    asked = [asks[0]] + [swap(asks[k], "hist", n_hist, k) for k in range(1, n_hist)]
    history = pl.pallas_call(
        load_kernel,
        out_shape=shape(history.shape),
        in_specs=[vmem()],
        out_specs=vmem(),
        compiler_params=params(),
        cost_estimate=cost(0, held * feature * 4),
        name="load",
    )(history)
    asked, those, history = lax.optimization_barrier((asked, wanted[:3], history))
    wanted = those + wanted[3:]

    fetched = pl.pallas_call(
        functools.partial(pull_kernel, n_hist, cap),
        out_shape=[shape((cap, feature))] * n_hist,
        in_specs=[vmem()] * (1 + n_hist),
        out_specs=[vmem()] * n_hist,
        compiler_params=params(),
        cost_estimate=cost(2 * n_hist * cap * held * feature, held * feature * 4),
        name="pull",
    )(history, *asked)
    arrived = [fetched[0]] + [swap(fetched[k], "hist", n_hist, k) for k in range(1, n_hist)]

    peers = range(1, n_half)
    soon = [k for k in peers if one_hop(k)]
    picked = pl.pallas_call(
        pick_own_kernel,
        out_shape=[shape((block_rows, feature))] * len(soon),
        in_specs=[vmem()] * (1 + len(soon)),
        out_specs=[vmem()] * len(soon),
        compiler_params=params(),
        cost_estimate=cost(0, n_half * 4 * block_rows * feature),
        name="pick_own",
    )(hidden, *[wanted[k] for k in soon])
    early = [swap(one, "blk", n_blk, k) for one, k in zip(picked, soon)]

    def pick_far(peers, name):
        return pl.pallas_call(
            functools.partial(pick_far_kernel, block_rows, peers),
            out_shape=[
                shape((2 * block_rows if k and not one_hop(k) else block_rows, feature)) for k in peers
            ],
            in_specs=[vmem(), vmem(), anywhere] + [vmem()] * len(peers),
            out_specs=[vmem()] * len(peers),
            compiler_params=params(),
            cost_estimate=cost(0, n_half * 4 * block_rows * feature),
            name=name,
        )(hidden, far, arrived[1], *[wanted[k] for k in peers])

    single = [k for k in range(n_half) if k & (k - 1) == 0]
    double = [k for k in range(n_half) if k & (k - 1)]
    picked = [None] * n_half
    for group, name in ((single, "pick_far"), (double, "pick_two_hop")):
        for k, one in zip(group, pick_far(group, name)):
            picked[k] = one
    mine = picked[0]
    late = [swap(picked[k], "blk", n_blk, k) for k in peers]

    spread = pl.pallas_call(
        functools.partial(spread_kernel, per_dev),
        out_shape=shape((n_blk, rows_dev, block_rows)),
        in_specs=[smem()] * 3 + [vmem(), anywhere],
        out_specs=vmem(),
        compiler_params=params(),
        cost_estimate=cost(0, n_blk * rows_dev * block_rows * 2),
        name="spread",
    )(place, tile_src, tile_dst, tiles, mine)

    part = pl.pallas_call(
        functools.partial(partial_kernel, n_hist, n_half, cap),
        out_shape=shape((rows_dev, feature), jnp.float32),
        in_specs=[vmem()] * (6 + n_hist + len(early)),
        out_specs=vmem(),
        compiler_params=params(),
        cost_estimate=cost(2 * rows_dev * feature * (rows_dev + n_hist * cap), rows_dev * feature * 12),
        name="partial",
    )(own_adj, hidden, pull_adj, initial, spread, mine, *arrived, *early)

    def final(chunks, name, first):
        rows = len(chunks) * per_owner
        return pl.pallas_call(
            functools.partial(final_kernel, n_half, chunks),
            out_shape=[shape((per_owner, feature))] * len(chunks),
            in_specs=[anywhere] + [vmem()] * (2 + n_half),
            out_specs=[vmem()] * len(chunks),
            scratch_shapes=[VMEM((rows, feature), jnp.float32), VMEM((rows, feature), jnp.bfloat16)],
            compiler_params=params(),
            cost_estimate=cost(2 * rows * feature * feature, rows * feature * 12),
            name=name,
        )(first, part, spread, weight, *late)

    outer = final(list(range(1, n_hist)), "final_sent", mine)
    inner = final([0], "final_kept", outer[0])
    sent = inner + outer
    pushed = [sent[0]] + [swap(sent[k], "hist", n_hist, k) for k in range(1, n_hist)]

    base, hot, refreshed = pl.pallas_call(
        functools.partial(prepare_kernel, n_hist, cap),
        out_shape=[shape((held, feature)), shape((held, rows_dev)), shape((rows_dev, feature))],
        in_specs=[vmem()] * (1 + 2 * n_hist),
        out_specs=[vmem(), vmem(), anywhere],
        scratch_shapes=[VMEM((1, rows_dev), jnp.int32), pltpu.SemaphoreType.DMA((n_hist,))],
        compiler_params=params(),
        cost_estimate=cost(held * rows_dev * 8, held * feature * 6),
        name="prepare",
    )(history, *asked, *sent)

    steps = 4
    pushed[2], pushed[1], pushed[3] = lax.optimization_barrier((pushed[2], pushed[1], pushed[3]))
    new_history = pl.pallas_call(
        functools.partial(scatter_kernel, steps),
        out_shape=shape((held, feature)),
        in_specs=[vmem()] * (2 + n_hist),
        out_specs=anywhere,
        scratch_shapes=[
            VMEM((rows_dev, feature), jnp.bfloat16),
            VMEM((held, feature), jnp.bfloat16),
            pltpu.SemaphoreType.DMA((steps,)),
        ],
        compiler_params=params(),
        name="scatter",
    )(base, hot, *pushed)
    return (refreshed, new_history)


def solution(mesh):
    both = P(("blk", "hist"))
    return jax.shard_map(
        local,
        mesh=mesh,
        in_specs=(both,) * 10 + (P(), both),
        out_specs=(both, both),
        check_vma=False,
    )
```

```python
import functools

import jax
import jax.numpy as jnp
from jax import lax
from jax.experimental import pallas as pl
from jax.experimental.pallas import tpu as pltpu
from jax.sharding import PartitionSpec as P

alpha_init = 0.1
beta_map = 0.4

VMEM = pltpu.VMEM
SMEM = pltpu.SMEM
LIMIT = 24 * 1024 * 1024


def vmem():
    return pl.BlockSpec(memory_space=VMEM)


def smem():
    return pl.BlockSpec(memory_space=SMEM)


def cost(flops, size):
    return pl.CostEstimate(flops=flops, bytes_accessed=size, transcendentals=0)


def params():
    return pltpu.CompilerParams(vmem_limit_bytes=LIMIT)


def swap(x, axis, n, k):
    return lax.ppermute(x, axis, [(i, i ^ k) for i in range(n)])


def message_kernel(n_hist, n_half, per_dev, after, src, count, rows, push, *outs):
    to_hist, to_half = outs[:n_hist], outs[n_hist:]
    cap = rows.shape[2]
    per_owner = push.shape[1] // n_hist
    b, h = lax.axis_index("blk"), lax.axis_index("hist")
    name = lax.div(src[...], per_dev) ^ b
    local = lax.rem(src[...], per_dev)
    for k in range(n_half):
        for slot, wanted in enumerate((k + n_half, k)):
            found = jnp.sum(jnp.where(name == wanted, local, 0), axis=1, keepdims=True)
            to_half[k][:, slot * 128 : slot * 128 + 128] = jnp.broadcast_to(found, (1, 128))
    owner = lax.broadcasted_iota(jnp.int32, count.shape, 1)
    lane = lax.broadcasted_iota(jnp.int32, (1, cap), 1)
    for k in range(n_hist):
        o = h ^ k
        used = jnp.sum(jnp.where(owner == o, count[...], 0), axis=1, keepdims=True)
        to_hist[k][:, :cap] = jnp.where(lane < used, rows[0, pl.ds(o, 1), :], -1)
        pushed = push[:, :per_owner]
        for j in range(1, n_hist):
            pushed = jnp.where(o == j, push[:, j * per_owner : (j + 1) * per_owner], pushed)
        to_hist[k][:, cap : cap + per_owner] = pushed


def pick(held, asked, slot, rows):
    wanted = asked[:, slot * 128 : slot * 128 + 1]
    block = held[:rows, :]
    for j in range(1, held.shape[0] // rows):
        block = jnp.where(
            jnp.broadcast_to(wanted == j, block.shape), held[j * rows : (j + 1) * rows, :], block
        )
    return block


def one_hop(k):
    return k > 1 and k & (k - 1) == 0


def pick_own_kernel(hidden, *refs):
    asked, outs = refs[: len(refs) // 2], refs[len(refs) // 2 :]
    for one, out in zip(asked, outs):
        out[...] = pick(hidden, one, 1, out.shape[0])


def pick_far_kernel(rows, peers, hidden, far, after, *refs):
    asked, outs = refs[: len(peers)], refs[len(peers) :]
    for one, out in zip(asked, outs):
        out[:rows, :] = pick(far, one, 0, rows)
        if out.shape[0] > rows:
            out[rows:, :] = pick(hidden, one, 1, rows)


def spread_kernel(per_dev, place, src, dst, tiles, after, out):
    block = tiles.shape[1]
    out[...] = jnp.zeros_like(out)
    for t in range(tiles.shape[0]):
        rows = pl.ds(pl.multiple_of(dst[0, t] * block, block), block)
        out[(src[0, t] // per_dev) ^ place[0], rows, :] = tiles[t]


def load_kernel(history, out):
    out[...] = history[...]


def pull_kernel(n_hist, cap, history, *refs):
    asked, outs = refs[:n_hist], refs[n_hist:]
    held = lax.broadcasted_iota(jnp.int32, (history.shape[0], cap), 0)
    for k in range(n_hist):
        hot = jnp.where(held == asked[k][:, :cap], 1.0, 0.0).astype(jnp.bfloat16)
        outs[k][...] = lax.dot_general(
            hot, history[...], (((0,), (0,)), ((), ())), preferred_element_type=jnp.float32
        ).astype(jnp.bfloat16)


def prepare_kernel(n_hist, cap, history, *refs):
    asked, sent = refs[:n_hist], refs[n_hist : 2 * n_hist]
    base, hot, refreshed, index, sem = refs[2 * n_hist :]
    h = lax.axis_index("hist")
    size = index.shape[1] // n_hist
    copies = []
    for k in range(n_hist):
        to = refreshed.at[pl.ds(pl.multiple_of((h ^ k) * size, size), size), :]
        copies.append(pltpu.make_async_copy(sent[k], to, sem.at[k]))
        copies[-1].start()
        index[:, k * size : (k + 1) * size] = asked[k][:, cap : cap + size]
    held = lax.broadcasted_iota(jnp.int32, hot.shape, 0)
    found = jnp.where(held == index[...], 1.0, 0.0)
    hot[...] = found.astype(jnp.bfloat16)
    hit = jnp.sum(found, axis=1, keepdims=True)
    base[...] = jnp.where(hit > 0.0, 0.0, history[...].astype(jnp.float32)).astype(jnp.bfloat16)
    for copy in copies:
        copy.wait()


def partial_kernel(n_hist, n_half, cap, own_adj, hidden, pull_adj, initial, spread, mine, *refs):
    arrived, early, out = refs[:n_hist], refs[n_hist:-1], refs[-1]
    h = lax.axis_index("hist")
    total = jnp.dot(own_adj[...], hidden[...], preferred_element_type=jnp.float32)
    total += jnp.dot(spread[n_half], mine[...], preferred_element_type=jnp.float32)
    for k, one in zip([k for k in range(n_half) if k and one_hop(k)], early):
        total += jnp.dot(spread[k], one[...], preferred_element_type=jnp.float32)
    for k in range(n_hist):
        columns = pl.ds(pl.multiple_of((h ^ k) * cap, cap), cap)
        total += jnp.dot(pull_adj[:, columns], arrived[k][...], preferred_element_type=jnp.float32)
    out[...] = (1.0 - alpha_init) * total + alpha_init * initial[...].astype(jnp.float32)


def final_kernel(n_half, chunks, first, part, spread, weight, *refs):
    late, sent, total, support = refs[: n_half - 1], refs[n_half - 1 : -2], refs[-2], refs[-1]
    block = spread.shape[2]
    size = sent[0].shape[0]
    for i, k in enumerate(chunks):
        rows = pl.ds(pl.multiple_of((lax.axis_index("hist") ^ k) * size, size), size)
        here = slice(i * size, (i + 1) * size)
        total[here, :] = part[rows, :]
        for j in range(1, n_half):
            total[here, :] += (1.0 - alpha_init) * jnp.dot(
                spread[n_half + j, rows, :], late[j - 1][:block, :], preferred_element_type=jnp.float32
            )
            if not one_hop(j):
                total[here, :] += (1.0 - alpha_init) * jnp.dot(
                    spread[j, rows, :], late[j - 1][block:, :], preferred_element_type=jnp.float32
                )
    support[...] = total[...].astype(jnp.bfloat16)
    projected = jnp.dot(support[...], weight[...], preferred_element_type=jnp.float32)
    result = jnp.maximum(
        (1.0 - beta_map) * support[...].astype(jnp.float32) + beta_map * projected, 0.0
    ).astype(jnp.bfloat16)
    for i in range(len(chunks)):
        sent[i][...] = result[i * size : (i + 1) * size, :]


def scatter_kernel(steps, base, hot, *refs):
    pushed, (out, rows, new, sem) = refs[:-4], refs[-4:]
    size = pushed[0].shape[0]
    for k, one in enumerate(pushed):
        rows[k * size : (k + 1) * size, :] = one[...]
    step = base.shape[0] // steps
    copies = []
    for i in range(steps):
        at = slice(i * step, (i + 1) * step)
        found = jnp.dot(hot[at, :], rows[...], preferred_element_type=jnp.float32)
        new[at, :] = (base[at, :].astype(jnp.float32) + found).astype(jnp.bfloat16)
        copies.append(pltpu.make_async_copy(new.at[at, :], out.at[at, :], sem.at[i]))
        copies[-1].start()
    for copy in copies:
        copy.wait()


def local(
    hidden,
    initial,
    own_adj,
    tiles,
    tile_src,
    tile_dst,
    history,
    pull_rows,
    pull_count,
    pull_adj,
    weight,
    push_rows,
):
    rows_dev, feature = hidden.shape
    block_rows = tiles.shape[1]
    per_dev = rows_dev // block_rows
    n_blk = lax.axis_size("blk")
    n_hist = lax.axis_size("hist")
    cap = pull_rows.shape[2]
    per_owner = rows_dev // n_hist
    held = history.shape[0]
    n_half = n_blk // 2
    place = jnp.stack([lax.axis_index("blk"), lax.axis_index("hist")]).astype(jnp.int32)
    anywhere = pl.BlockSpec(memory_space=pl.ANY)

    def shape(s, dtype=jnp.bfloat16):
        return jax.ShapeDtypeStruct(s, dtype)

    far = swap(hidden, "blk", n_blk, n_half)
    asks = pl.pallas_call(
        functools.partial(message_kernel, n_hist, n_half, per_dev),
        out_shape=[shape((1, cap + 128), jnp.int32)] * n_hist
        + [shape((1, 256), jnp.int32) for k in range(n_half)],
        in_specs=[anywhere] + [vmem()] * 4,
        out_specs=[vmem()] * (n_hist + n_half),
        compiler_params=params(),
        name="message",
    )(place, tile_src, pull_count, pull_rows, push_rows.reshape(1, rows_dev))
    wanted = [asks[n_hist]] + [swap(asks[n_hist + k], "blk", n_blk, k) for k in range(1, n_half)]
    asked = [asks[0]] + [swap(asks[k], "hist", n_hist, k) for k in range(1, n_hist)]
    history = pl.pallas_call(
        load_kernel,
        out_shape=shape(history.shape),
        in_specs=[vmem()],
        out_specs=vmem(),
        compiler_params=params(),
        cost_estimate=cost(0, held * feature * 4),
        name="load",
    )(history)
    ones = [k for k in range(1, n_half) if k & (k - 1) == 0]
    first = [asked[1], wanted[1], *asked[2:], *[wanted[k] for k in ones[1:]]]
    asked[0], wanted[0], first, history = lax.optimization_barrier(
        (asked[0], wanted[0], first, history)
    )
    asked[1:], wanted[1] = [first[0], *first[2 : n_hist]], first[1]
    for k, one in zip(ones[1:], first[n_hist:]):
        wanted[k] = one

    fetched = pl.pallas_call(
        functools.partial(pull_kernel, n_hist, cap),
        out_shape=[shape((cap, feature))] * n_hist,
        in_specs=[vmem()] * (1 + n_hist),
        out_specs=[vmem()] * n_hist,
        compiler_params=params(),
        cost_estimate=cost(2 * n_hist * cap * held * feature, held * feature * 4),
        name="pull",
    )(history, *asked)
    arrived = [fetched[0]] + [swap(fetched[k], "hist", n_hist, k) for k in range(1, n_hist)]

    peers = range(1, n_half)
    soon = [k for k in peers if one_hop(k)]
    picked = pl.pallas_call(
        pick_own_kernel,
        out_shape=[shape((block_rows, feature))] * len(soon),
        in_specs=[vmem()] * (1 + len(soon)),
        out_specs=[vmem()] * len(soon),
        compiler_params=params(),
        cost_estimate=cost(0, n_half * 4 * block_rows * feature),
        name="pick_own",
    )(hidden, *[wanted[k] for k in soon])
    early = [swap(one, "blk", n_blk, k) for one, k in zip(picked, soon)]

    def pick_far(peers, name):
        return pl.pallas_call(
            functools.partial(pick_far_kernel, block_rows, peers),
            out_shape=[
                shape((2 * block_rows if k and not one_hop(k) else block_rows, feature)) for k in peers
            ],
            in_specs=[vmem(), vmem(), anywhere] + [vmem()] * len(peers),
            out_specs=[vmem()] * len(peers),
            compiler_params=params(),
            cost_estimate=cost(0, n_half * 4 * block_rows * feature),
            name=name,
        )(hidden, far, arrived[1], *[wanted[k] for k in peers])

    single = [k for k in range(n_half) if k & (k - 1) == 0]
    double = [k for k in range(n_half) if k & (k - 1)]
    picked = [None] * n_half
    for group, name in ((single, "pick_far"), (double, "pick_two_hop")):
        for k, one in zip(group, pick_far(group, name)):
            picked[k] = one
    mine = picked[0]
    late = [swap(picked[k], "blk", n_blk, k) for k in peers]

    spread = pl.pallas_call(
        functools.partial(spread_kernel, per_dev),
        out_shape=shape((n_blk, rows_dev, block_rows)),
        in_specs=[smem()] * 3 + [vmem(), anywhere],
        out_specs=vmem(),
        compiler_params=params(),
        cost_estimate=cost(0, n_blk * rows_dev * block_rows * 2),
        name="spread",
    )(place, tile_src, tile_dst, tiles, mine)

    part = pl.pallas_call(
        functools.partial(partial_kernel, n_hist, n_half, cap),
        out_shape=shape((rows_dev, feature), jnp.float32),
        in_specs=[vmem()] * (6 + n_hist + len(early)),
        out_specs=vmem(),
        compiler_params=params(),
        cost_estimate=cost(2 * rows_dev * feature * (rows_dev + n_hist * cap), rows_dev * feature * 12),
        name="partial",
    )(own_adj, hidden, pull_adj, initial, spread, mine, *arrived, *early)

    def final(chunks, name, first):
        rows = len(chunks) * per_owner
        return pl.pallas_call(
            functools.partial(final_kernel, n_half, chunks),
            out_shape=[shape((per_owner, feature))] * len(chunks),
            in_specs=[anywhere] + [vmem()] * (2 + n_half),
            out_specs=[vmem()] * len(chunks),
            scratch_shapes=[VMEM((rows, feature), jnp.float32), VMEM((rows, feature), jnp.bfloat16)],
            compiler_params=params(),
            cost_estimate=cost(2 * rows * feature * feature, rows * feature * 12),
            name=name,
        )(first, part, spread, weight, *late)

    outer = final(list(range(1, n_hist)), "final_sent", mine)
    inner = final([0], "final_kept", outer[0])
    sent = inner + outer
    pushed = [sent[0]] + [swap(sent[k], "hist", n_hist, k) for k in range(1, n_hist)]

    base, hot, refreshed = pl.pallas_call(
        functools.partial(prepare_kernel, n_hist, cap),
        out_shape=[shape((held, feature)), shape((held, rows_dev)), shape((rows_dev, feature))],
        in_specs=[vmem()] * (1 + 2 * n_hist),
        out_specs=[vmem(), vmem(), anywhere],
        scratch_shapes=[VMEM((1, rows_dev), jnp.int32), pltpu.SemaphoreType.DMA((n_hist,))],
        compiler_params=params(),
        cost_estimate=cost(held * rows_dev * 8, held * feature * 6),
        name="prepare",
    )(history, *asked, *sent)

    steps = 4
    outer, inner, *rest = lax.optimization_barrier((pushed[2], pushed[1], *pushed[3:]))
    pushed = [pushed[0], inner, outer, *rest]
    new_history = pl.pallas_call(
        functools.partial(scatter_kernel, steps),
        out_shape=shape((held, feature)),
        in_specs=[vmem()] * (2 + n_hist),
        out_specs=anywhere,
        scratch_shapes=[
            VMEM((rows_dev, feature), jnp.bfloat16),
            VMEM((held, feature), jnp.bfloat16),
            pltpu.SemaphoreType.DMA((steps,)),
        ],
        compiler_params=params(),
        name="scatter",
    )(base, hot, *pushed)
    return (refreshed, new_history)


def solution(mesh):
    both = P(("blk", "hist"))
    return jax.shard_map(
        local,
        mesh=mesh,
        in_specs=(both,) * 10 + (P(), both),
        out_specs=(both, both),
        check_vma=False,
    )
```

```python
import functools

import jax
import jax.numpy as jnp
from jax import lax
from jax.experimental import pallas as pl
from jax.experimental.pallas import tpu as pltpu
from jax.sharding import PartitionSpec as P

alpha_init = 0.1
beta_map = 0.4

VMEM = pltpu.VMEM
SMEM = pltpu.SMEM
LIMIT = 24 * 1024 * 1024


def vmem():
    return pl.BlockSpec(memory_space=VMEM)


def smem():
    return pl.BlockSpec(memory_space=SMEM)


def cost(flops, size):
    return pl.CostEstimate(flops=flops, bytes_accessed=size, transcendentals=0)


def params():
    return pltpu.CompilerParams(vmem_limit_bytes=LIMIT)


def swap(x, axis, n, k):
    return lax.ppermute(x, axis, [(i, i ^ k) for i in range(n)])


def message_kernel(n_hist, n_half, per_dev, after, src, count, rows, push, *outs):
    to_hist, to_half = outs[:n_hist], outs[n_hist:]
    cap = rows.shape[2]
    per_owner = push.shape[1] // n_hist
    b, h = lax.axis_index("blk"), lax.axis_index("hist")
    name = lax.div(src[...], per_dev) ^ b
    local = lax.rem(src[...], per_dev)
    for k in range(n_half):
        for slot, wanted in enumerate((k + n_half, k)):
            found = jnp.sum(jnp.where(name == wanted, local, 0), axis=1, keepdims=True)
            at = k % 2 * 256 + slot * 128
            to_half[k // 2][:, at : at + 128] = jnp.broadcast_to(found, (1, 128))
    owner = lax.broadcasted_iota(jnp.int32, count.shape, 1)
    lane = lax.broadcasted_iota(jnp.int32, (1, cap), 1)
    for k in range(n_hist):
        o = h ^ k
        used = jnp.sum(jnp.where(owner == o, count[...], 0), axis=1, keepdims=True)
        to_hist[k][:, :cap] = jnp.where(lane < used, rows[0, pl.ds(o, 1), :], -1)
        pushed = push[:, :per_owner]
        for j in range(1, n_hist):
            pushed = jnp.where(o == j, push[:, j * per_owner : (j + 1) * per_owner], pushed)
        to_hist[k][:, cap : cap + per_owner] = pushed


def pick(held, asked, k, slot, rows):
    at = k % 2 * 256 + slot * 128
    wanted = asked[:, at : at + 1]
    block = held[:rows, :]
    for j in range(1, held.shape[0] // rows):
        block = jnp.where(
            jnp.broadcast_to(wanted == j, block.shape), held[j * rows : (j + 1) * rows, :], block
        )
    return block


def one_hop(k):
    return False


def pick_far_kernel(rows, peers, hidden, far, after, *refs):
    asked, outs = refs[: len(peers)], refs[len(peers) :]
    for k, one, out in zip(peers, asked, outs):
        out[:rows, :] = pick(far, one, k, 0, rows)
        if out.shape[0] > rows:
            out[rows:, :] = pick(hidden, one, k, 1, rows)


def spread_kernel(per_dev, place, src, dst, tiles, after, out):
    block = tiles.shape[1]
    out[...] = jnp.zeros_like(out)
    for t in range(tiles.shape[0]):
        rows = pl.ds(pl.multiple_of(dst[0, t] * block, block), block)
        out[(src[0, t] // per_dev) ^ place[0], rows, :] = tiles[t]


def load_kernel(history, out):
    out[...] = history[...]


def pull_kernel(n_hist, cap, history, *refs):
    asked, outs = refs[:n_hist], refs[n_hist:]
    held = lax.broadcasted_iota(jnp.int32, (history.shape[0], cap), 0)
    for k in range(n_hist):
        hot = jnp.where(held == asked[k][:, :cap], 1.0, 0.0).astype(jnp.bfloat16)
        outs[k][...] = lax.dot_general(
            hot, history[...], (((0,), (0,)), ((), ())), preferred_element_type=jnp.float32
        ).astype(jnp.bfloat16)


def prepare_kernel(n_hist, cap, history, *refs):
    asked, sent = refs[:n_hist], refs[n_hist : 2 * n_hist]
    base, hot, refreshed, index, sem = refs[2 * n_hist :]
    h = lax.axis_index("hist")
    size = index.shape[1] // n_hist
    copies = []
    for k in range(n_hist):
        to = refreshed.at[pl.ds(pl.multiple_of((h ^ k) * size, size), size), :]
        copies.append(pltpu.make_async_copy(sent[k], to, sem.at[k]))
        copies[-1].start()
        index[:, k * size : (k + 1) * size] = asked[k][:, cap : cap + size]
    held = lax.broadcasted_iota(jnp.int32, hot.shape, 0)
    found = jnp.where(held == index[...], 1.0, 0.0)
    hot[...] = found.astype(jnp.bfloat16)
    hit = jnp.sum(found, axis=1, keepdims=True)
    base[...] = jnp.where(hit > 0.0, 0.0, history[...].astype(jnp.float32)).astype(jnp.bfloat16)
    for copy in copies:
        copy.wait()


def partial_kernel(n_hist, n_half, cap, own_adj, hidden, pull_adj, initial, spread, mine, *refs):
    arrived, early, out = refs[:n_hist], refs[n_hist:-1], refs[-1]
    h = lax.axis_index("hist")
    total = jnp.dot(own_adj[...], hidden[...], preferred_element_type=jnp.float32)
    total += jnp.dot(spread[n_half], mine[...], preferred_element_type=jnp.float32)
    for k, one in zip([k for k in range(n_half) if k and one_hop(k)], early):
        total += jnp.dot(spread[k], one[...], preferred_element_type=jnp.float32)
    for k in range(n_hist):
        columns = pl.ds(pl.multiple_of((h ^ k) * cap, cap), cap)
        total += jnp.dot(pull_adj[:, columns], arrived[k][...], preferred_element_type=jnp.float32)
    out[...] = (1.0 - alpha_init) * total + alpha_init * initial[...].astype(jnp.float32)


def final_kernel(n_half, chunks, first, part, spread, weight, *refs):
    late, sent, total, support = refs[: n_half - 1], refs[n_half - 1 : -2], refs[-2], refs[-1]
    block = spread.shape[2]
    size = sent[0].shape[0]
    for i, k in enumerate(chunks):
        rows = pl.ds(pl.multiple_of((lax.axis_index("hist") ^ k) * size, size), size)
        here = slice(i * size, (i + 1) * size)
        total[here, :] = part[rows, :]
        for j in range(1, n_half):
            total[here, :] += (1.0 - alpha_init) * jnp.dot(
                spread[n_half + j, rows, :], late[j - 1][:block, :], preferred_element_type=jnp.float32
            )
            if not one_hop(j):
                total[here, :] += (1.0 - alpha_init) * jnp.dot(
                    spread[j, rows, :], late[j - 1][block:, :], preferred_element_type=jnp.float32
                )
    support[...] = total[...].astype(jnp.bfloat16)
    projected = jnp.dot(support[...], weight[...], preferred_element_type=jnp.float32)
    result = jnp.maximum(
        (1.0 - beta_map) * support[...].astype(jnp.float32) + beta_map * projected, 0.0
    ).astype(jnp.bfloat16)
    for i in range(len(chunks)):
        sent[i][...] = result[i * size : (i + 1) * size, :]


def scatter_kernel(steps, base, hot, *refs):
    pushed, (out, rows, new, sem) = refs[:-4], refs[-4:]
    size = pushed[0].shape[0]
    for k, one in enumerate(pushed):
        rows[k * size : (k + 1) * size, :] = one[...]
    step = base.shape[0] // steps
    copies = []
    for i in range(steps):
        at = slice(i * step, (i + 1) * step)
        found = jnp.dot(hot[at, :], rows[...], preferred_element_type=jnp.float32)
        new[at, :] = (base[at, :].astype(jnp.float32) + found).astype(jnp.bfloat16)
        copies.append(pltpu.make_async_copy(new.at[at, :], out.at[at, :], sem.at[i]))
        copies[-1].start()
    for copy in copies:
        copy.wait()


def local(
    hidden,
    initial,
    own_adj,
    tiles,
    tile_src,
    tile_dst,
    history,
    pull_rows,
    pull_count,
    pull_adj,
    weight,
    push_rows,
):
    rows_dev, feature = hidden.shape
    block_rows = tiles.shape[1]
    per_dev = rows_dev // block_rows
    n_blk = lax.axis_size("blk")
    n_hist = lax.axis_size("hist")
    cap = pull_rows.shape[2]
    per_owner = rows_dev // n_hist
    held = history.shape[0]
    n_half = n_blk // 2
    place = jnp.stack([lax.axis_index("blk"), lax.axis_index("hist")]).astype(jnp.int32)
    anywhere = pl.BlockSpec(memory_space=pl.ANY)

    def shape(s, dtype=jnp.bfloat16):
        return jax.ShapeDtypeStruct(s, dtype)

    far = swap(hidden, "blk", n_blk, n_half)
    asks = pl.pallas_call(
        functools.partial(message_kernel, n_hist, n_half, per_dev),
        out_shape=[shape((1, cap + 128), jnp.int32)] * n_hist
        + [shape((1, 512), jnp.int32)] * (n_half // 2),
        in_specs=[anywhere] + [vmem()] * 4,
        out_specs=[vmem()] * (n_hist + n_half // 2),
        compiler_params=params(),
        name="message",
    )(place, tile_src, pull_count, pull_rows, push_rows.reshape(1, rows_dev))
    came = [asks[n_hist]]
    came += [swap(asks[n_hist + k // 2], "blk", n_blk, k) for k in range(2, n_half, 2)]
    wanted = [None] * n_half
    wanted[0::2] = came
    wanted[1] = swap(came[0], "blk", n_blk, 1)
    asked = [asks[0]] + [swap(asks[k], "hist", n_hist, k) for k in range(1, n_hist)]
    history = pl.pallas_call(
        load_kernel,
        out_shape=shape(history.shape),
        in_specs=[vmem()],
        out_specs=vmem(),
        compiler_params=params(),
        cost_estimate=cost(0, held * feature * 4),
        name="load",
    )(history)
    ones = [1, *range(2, n_half, 2)]
    first = [asked[1], wanted[1], *asked[2:], *[wanted[k] for k in ones[1:]]]
    asked[0], wanted[0], first, history = lax.optimization_barrier(
        (asked[0], wanted[0], first, history)
    )
    asked[1:], wanted[1] = [first[0], *first[2 : n_hist]], first[1]
    for k, one in zip(ones[1:], first[n_hist:]):
        wanted[k] = one
    wanted[3::2] = [swap(one, "blk", n_blk, 1) for one in wanted[2::2]]

    fetched = pl.pallas_call(
        functools.partial(pull_kernel, n_hist, cap),
        out_shape=[shape((cap, feature))] * n_hist,
        in_specs=[vmem()] * (1 + n_hist),
        out_specs=[vmem()] * n_hist,
        compiler_params=params(),
        cost_estimate=cost(2 * n_hist * cap * held * feature, held * feature * 4),
        name="pull",
    )(history, *asked)
    arrived = [fetched[0]] + [swap(fetched[k], "hist", n_hist, k) for k in range(1, n_hist)]

    peers = range(1, n_half)
    soon = [k for k in peers if one_hop(k)]
    picked = []
    early = [swap(one, "blk", n_blk, k) for one, k in zip(picked, soon)]

    def pick_far(peers, name):
        return pl.pallas_call(
            functools.partial(pick_far_kernel, block_rows, peers),
            out_shape=[
                shape((2 * block_rows if k and not one_hop(k) else block_rows, feature)) for k in peers
            ],
            in_specs=[vmem(), vmem(), anywhere] + [vmem()] * len(peers),
            out_specs=[vmem()] * len(peers),
            compiler_params=params(),
            cost_estimate=cost(0, n_half * 4 * block_rows * feature),
            name=name,
        )(hidden, far, arrived[1], *[wanted[k] for k in peers])

    single = [k for k in range(n_half) if k & (k - 1) == 0]
    double = [k for k in range(n_half) if k & (k - 1)]
    picked = [None] * n_half
    for group, name in ((single, "pick_far"), (double, "pick_two_hop")):
        for k, one in zip(group, pick_far(group, name)):
            picked[k] = one
    mine = picked[0]
    late = [swap(picked[k], "blk", n_blk, k) for k in peers]

    spread = pl.pallas_call(
        functools.partial(spread_kernel, per_dev),
        out_shape=shape((n_blk, rows_dev, block_rows)),
        in_specs=[smem()] * 3 + [vmem(), anywhere],
        out_specs=vmem(),
        compiler_params=params(),
        cost_estimate=cost(0, n_blk * rows_dev * block_rows * 2),
        name="spread",
    )(place, tile_src, tile_dst, tiles, mine)

    late[1], late[0], late[2] = lax.optimization_barrier((late[1], late[0], late[2]))
    part = pl.pallas_call(
        functools.partial(partial_kernel, n_hist, n_half, cap),
        out_shape=shape((rows_dev, feature), jnp.float32),
        in_specs=[vmem()] * (6 + n_hist + len(early)),
        out_specs=vmem(),
        compiler_params=params(),
        cost_estimate=cost(2 * rows_dev * feature * (rows_dev + n_hist * cap), rows_dev * feature * 12),
        name="partial",
    )(own_adj, hidden, pull_adj, initial, spread, mine, *arrived, *early)

    def final(chunks, name, first):
        rows = len(chunks) * per_owner
        return pl.pallas_call(
            functools.partial(final_kernel, n_half, chunks),
            out_shape=[shape((per_owner, feature))] * len(chunks),
            in_specs=[anywhere] + [vmem()] * (2 + n_half),
            out_specs=[vmem()] * len(chunks),
            scratch_shapes=[VMEM((rows, feature), jnp.float32), VMEM((rows, feature), jnp.bfloat16)],
            compiler_params=params(),
            cost_estimate=cost(2 * rows * feature * feature, rows * feature * 12),
            name=name,
        )(first, part, spread, weight, *late)

    outer = final(list(range(1, n_hist)), "final_sent", mine)
    inner = final([0], "final_kept", outer[0])
    sent = inner + outer
    pushed = [sent[0]] + [swap(sent[k], "hist", n_hist, k) for k in range(1, n_hist)]

    base, hot, refreshed = pl.pallas_call(
        functools.partial(prepare_kernel, n_hist, cap),
        out_shape=[shape((held, feature)), shape((held, rows_dev)), shape((rows_dev, feature))],
        in_specs=[vmem()] * (1 + 2 * n_hist),
        out_specs=[vmem(), vmem(), anywhere],
        scratch_shapes=[VMEM((1, rows_dev), jnp.int32), pltpu.SemaphoreType.DMA((n_hist,))],
        compiler_params=params(),
        cost_estimate=cost(held * rows_dev * 8, held * feature * 6),
        name="prepare",
    )(history, *asked, *sent)

    steps = 4
    outer, inner, *rest = lax.optimization_barrier((pushed[2], pushed[1], *pushed[3:]))
    pushed = [pushed[0], inner, outer, *rest]
    new_history = pl.pallas_call(
        functools.partial(scatter_kernel, steps),
        out_shape=shape((held, feature)),
        in_specs=[vmem()] * (2 + n_hist),
        out_specs=anywhere,
        scratch_shapes=[
            VMEM((rows_dev, feature), jnp.bfloat16),
            VMEM((held, feature), jnp.bfloat16),
            pltpu.SemaphoreType.DMA((steps,)),
        ],
        compiler_params=params(),
        name="scatter",
    )(base, hot, *pushed)
    return (refreshed, new_history)


def solution(mesh):
    both = P(("blk", "hist"))
    return jax.shard_map(
        local,
        mesh=mesh,
        in_specs=(both,) * 10 + (P(), both),
        out_specs=(both, both),
        check_vma=False,
    )
```
